32 devices in a mesh: group: 2 (over x), frame: 16 (over z, y, core).
Axes of the slice: x: 2, y: 2, z: 4, core: 2. Of those that a mesh axis runs over, the one named last changes fastest.
Arguments:
- queries: bfloat16 [10240, 5120], P(('group', 'frame')), parts along dimension 0, may hold values from -33 to 33
- keys: bfloat16 [10240, 5120], P(('group', 'frame')), parts along dimension 0, may hold values from -33 to 33
- values: bfloat16 [10240, 5120], P(('group', 'frame')), parts along dimension 0, may hold values from -6 to 6
- labels: int32 [80], P('group'), parts along dimension 0, may hold values from 0 to 1, as said below
- band: int32 [80], P('group'), parts along dimension 0, may hold values from 2 to 4
Outputs:
- attended: bfloat16 [10240, 5120], P(('group', 'frame')), parts along dimension 0
The draws below stay inside these ranges and needn't reach their ends.
There are 2 independent parts, one for each index of `group`. The reference program is written for one: setup_inputs(seed, part) draws one part's arguments, and reference() takes and returns one part's arrays. A program takes and returns all parts, laid end to end along the dimension named above; each array names one. Nothing has to cross between parts.
Inputs may be any that keep to these rules, and one draw needn't show every extreme that they name: `labels`: exactly 10 of the 40 heads carry 1, the others 0.
All inputs are finite; a program needn't handle non-finite values.
Results may differ from the reference program's by a relative error of at most 0.0049.
Values may be sent and summed in bfloat16 or wider, within the bound.
No kernel may reach another device: no remote copies, remote signals or barrier semaphores. Data moves between devices by JAX's collectives and lax.ppermute only.
A program may use at most 128 MiB of HBM per device.

```python
import math
import jax
import jax.numpy as jnp
from jax import lax

HEADS = 40
HEAD_DIM = 128
TEMP_HEADS = 10
FRAMES = 8
FPIX = 640
TOKENS = 5120
WIDTH = 5120


def drawn_rows(key):
    return jnp.clip(jax.random.normal(key, (TOKENS, HEADS * HEAD_DIM), jnp.float32), -6.0, 6.0)


def draw_queries(key, part):
    result = drawn_rows(jax.random.fold_in(key, 1))
    return result.astype(jnp.bfloat16)


def draw_keys(key, part):
    result = drawn_rows(jax.random.fold_in(key, 2))
    return result.astype(jnp.bfloat16)


def draw_labels(key, part):
    order = jax.random.permutation(key, HEADS)
    return (order < TEMP_HEADS).astype(jnp.int32)


def set_ends(array, key, smallest, largest):
    extent = array.shape
    spot = [jax.random.randint(jax.random.fold_in(key, axis), (), 0, extent[axis]) for axis in range(len(extent))]
    array = array.at[tuple(spot)].set(smallest)
    longest = extent.index(max(extent))
    spot[longest] = (spot[longest] + 1) % extent[longest]
    return array.at[tuple(spot)].set(largest)


def block_scale(stream_key, dims, cuts, low, top_value):
    gain = 1.0
    for axis_at, blocks in cuts:
        heights = jax.random.uniform(jax.random.fold_in(jax.random.fold_in(stream_key, 6), axis_at), (blocks,), jnp.float32, low / len(cuts), top_value / len(cuts))
        gain = gain * jnp.repeat(jnp.exp(heights), dims[axis_at] // blocks).reshape((-1,) + (1,) * (len(dims) - 1 - axis_at))
    return gain


def normal_values(stream_key, dims, width, reach, cuts=(), held_as=jnp.bfloat16):
    factor_of = block_scale(stream_key, dims, cuts, -0.22, 0.18) if cuts else 1.0
    values = jax.random.normal(stream_key, dims, jnp.float32) * width * factor_of
    return jnp.minimum(jnp.maximum(values, -reach), reach).astype(held_as)


def setup_inputs(seed: int = 0, part: int = 0) -> dict:
    key_list = jax.random.split(jax.random.key(seed), 6)
    part_keys = jax.random.split(jax.random.fold_in(key_list[5], part), 6)
    queries = draw_queries(jax.random.fold_in(jax.random.fold_in(key_list[5], part), 71), part)
    keys = draw_keys(jax.random.fold_in(jax.random.fold_in(key_list[5], part), 71), part)
    values = normal_values(part_keys[2], (TOKENS, WIDTH), 1.0, 6.0, ((0, 16),))
    labels = draw_labels(jax.random.fold_in(jax.random.fold_in(key_list[5], part), 71), part)
    band = set_ends(jax.random.randint(part_keys[4], (HEADS,), FRAMES // 4, FRAMES // 2 + 1), jax.random.fold_in(part_keys[4], 1), FRAMES // 4, (FRAMES // 2 + 1) - 1).astype(jnp.int32)
    return dict(queries=queries, keys=keys, values=values, labels=labels, band=band)


def softmax_rounded(scores):
    peak = lax.optimization_barrier(jnp.max(scores, axis=-1, keepdims=True))
    weights = jnp.exp(scores - peak)
    return (weights / lax.optimization_barrier(jnp.sum(weights, axis=-1, keepdims=True))).astype(jnp.bfloat16)

def reference(queries, keys, values, labels, band):
    scale = 1.0 / math.sqrt(HEAD_DIM)
    grid_shape = (FRAMES, FPIX, HEADS, HEAD_DIM)
    query_grid = queries.reshape(grid_shape)
    key_grid = keys.reshape(grid_shape)
    value_grid = values.reshape(grid_shape)

    def one_frame(pieces):
        query_frame, key_frame, value_frame = pieces
        scores = jnp.einsum('phd,khd->hpk', query_frame.astype(jnp.float32), key_frame.astype(jnp.float32)) * scale
        weights = softmax_rounded(scores)
        return jnp.einsum('hpk,khd->phd', weights.astype(jnp.float32), value_frame.astype(jnp.float32)).astype(jnp.bfloat16)
    spatial = lax.map(one_frame, (query_grid, key_grid, value_grid))
    frame_ids = jnp.arange(FRAMES, dtype=jnp.int32)
    distance = jnp.abs(frame_ids[:, None] - frame_ids[None, :])

    def one_head(pieces):
        query_head, key_head, value_head, head_band = pieces
        keep = distance <= head_band
        scores = jnp.einsum('fpd,gpd->pfg', query_head.astype(jnp.float32), key_head.astype(jnp.float32)) * scale
        scores = jnp.where(keep[None], scores, jnp.float32(-1e+30))
        weights = softmax_rounded(scores)
        return jnp.einsum('pfg,gpd->fpd', weights.astype(jnp.float32), value_head.astype(jnp.float32)).astype(jnp.bfloat16)
    temporal = lax.map(one_head, (jnp.moveaxis(query_grid, 2, 0), jnp.moveaxis(key_grid, 2, 0), jnp.moveaxis(value_grid, 2, 0), band))
    temporal = jnp.moveaxis(temporal, 0, 2)
    chosen = jnp.where((labels == 1)[None, None, :, None], temporal, spatial)
    return chosen.reshape(TOKENS, HEADS * HEAD_DIM)
```

```python
import functools
import math

import jax
import jax.numpy as jnp
from jax import lax
from jax.experimental import pallas as pl
from jax.experimental.pallas import tpu as pltpu
from jax.sharding import PartitionSpec as P

TEMP_HEADS = 10
HEAD_DIM = 128
PIXEL_BLOCK = 32
SPATIAL_PIECES = 3
MASKED = -1e30
VMEM_BYTES = 48 * 1024 * 1024


def swap_bit(block, bit):
    count = lax.axis_size("frame")
    return lax.ppermute(block, "frame", [(i, i ^ (1 << bit)) for i in range(count)])


def shift_pairs(block, step):
    count = lax.axis_size("frame")
    route = [(i, i + 4 * step) for i in range(count) if 0 <= i + 4 * step < count]
    return lax.ppermute(block, "frame", route)


def extract_kernel(
    place, labels, band, queries, keys, values,
    meta, pair_keep, pair_send, query_keep, query_send, sems,
):
    heads = labels.shape[0]
    half = query_keep.shape[1]
    side = place[0]

    def one_head(head, counts):
        spatial, temporal = counts
        is_temporal = labels[head] == 1

        @pl.when(is_temporal)
        def _():
            meta[heads + temporal] = head
            meta[2 * heads + temporal] = band[head]
            columns = pl.ds(pl.multiple_of(head * HEAD_DIM, HEAD_DIM), HEAD_DIM)
            kept = pl.ds(pl.multiple_of(side * half, half), half)
            sent = pl.ds(pl.multiple_of((1 - side) * half, half), half)
            for number, source in enumerate((keys, values)):
                pltpu.make_async_copy(source.at[kept, columns], pair_keep.at[number, temporal], sems.at[0]).start()
                pltpu.make_async_copy(source.at[sent, columns], pair_send.at[number, temporal], sems.at[1]).start()
            pltpu.make_async_copy(queries.at[kept, columns], query_keep.at[temporal], sems.at[2]).start()
            pltpu.make_async_copy(queries.at[sent, columns], query_send.at[temporal], sems.at[3]).start()

        @pl.when(jnp.logical_not(is_temporal))
        def _():
            meta[spatial] = head

        step = is_temporal.astype(jnp.int32)
        return spatial + 1 - step, temporal + step

    lax.fori_loop(0, heads, one_head, (jnp.int32(0), jnp.int32(0)))
    for number, whole in enumerate((pair_keep, pair_send, query_keep, query_send)):
        pltpu.make_async_copy(whole, whole, sems.at[number]).wait()


def extract(place, labels, band, queries, keys, values):
    rows = queries.shape[0]
    half = rows // 2
    pair = jax.ShapeDtypeStruct((2, TEMP_HEADS, half, HEAD_DIM), jnp.bfloat16)
    single = jax.ShapeDtypeStruct((TEMP_HEADS, half, HEAD_DIM), jnp.bfloat16)
    any_spec = pl.BlockSpec(memory_space=pl.ANY)
    smem_spec = pl.BlockSpec(memory_space=pltpu.SMEM)
    return pl.pallas_call(
        extract_kernel,
        out_shape=(jax.ShapeDtypeStruct((3 * labels.shape[0],), jnp.int32), pair, pair, single, single),
        in_specs=[smem_spec] * 3 + [any_spec] * 3,
        out_specs=(smem_spec,) + (any_spec,) * 4,
        scratch_shapes=[pltpu.SemaphoreType.DMA((4,))],
        cost_estimate=pl.CostEstimate(flops=0, bytes_accessed=12 * TEMP_HEADS * half * HEAD_DIM * 2, transcendentals=0),
        name="extract_temporal",
    )(place, labels, band, queries, keys, values)


def spatial_kernel(scale, meta, query, key_own, value_own, key_far, value_far, *rest):
    out, key_all, value_all = rest[-3:]
    rows = query.shape[0]
    key_all[:rows, :] = key_own[...]
    key_all[rows:, :] = key_far[...]
    value_all[:rows, :HEAD_DIM] = value_own[...]
    value_all[rows:, :HEAD_DIM] = value_far[...]
    value_all[:, HEAD_DIM:] = jnp.ones((2 * rows, HEAD_DIM), jnp.bfloat16)
    chunk = 64
    for start in range(0, rows, chunk):
        scores = lax.dot_general(
            query[start : start + chunk, :], key_all[...], (((1,), (1,)), ((), ())), preferred_element_type=jnp.float32
        )
        peak = jnp.max(scores, axis=1, keepdims=True)
        weights = jnp.exp2((scores - peak) * scale).astype(jnp.bfloat16)
        both = jnp.dot(weights, value_all[...], preferred_element_type=jnp.float32)
        out[start : start + chunk, :] = (both[:, :HEAD_DIM] / both[:, HEAD_DIM:]).astype(jnp.bfloat16)


def spatial_piece(meta, first, count, queries, keys, values, keys_far, values_far, so_far):
    rows = queries.shape[0]
    block = pl.BlockSpec((rows, HEAD_DIM), lambda i, meta: (0, meta[first + i]))
    operands = [queries, keys, values, keys_far, values_far]
    specs = [block] * 5
    aliases = {}
    if so_far is not None:
        operands.append(so_far)
        specs.append(pl.BlockSpec(memory_space=pl.ANY))
        aliases = {6: 0}
    return pl.pallas_call(
        functools.partial(spatial_kernel, math.log2(math.e) / math.sqrt(HEAD_DIM)),
        out_shape=jax.ShapeDtypeStruct(queries.shape, jnp.bfloat16),
        grid_spec=pltpu.PrefetchScalarGridSpec(
            num_scalar_prefetch=1,
            grid=(count,),
            in_specs=specs,
            out_specs=block,
            scratch_shapes=[
                pltpu.VMEM((2 * rows, HEAD_DIM), jnp.bfloat16),
                pltpu.VMEM((2 * rows, 2 * HEAD_DIM), jnp.bfloat16),
            ],
        ),
        input_output_aliases=aliases,
        compiler_params=pltpu.CompilerParams(vmem_limit_bytes=VMEM_BYTES),
        cost_estimate=pl.CostEstimate(
            flops=count * rows * 2 * rows * HEAD_DIM * 2 * 3,
            bytes_accessed=count * 6 * rows * HEAD_DIM * 2,
            transcendentals=count * rows * 2 * rows,
        ),
        name="spatial_heads",
    )(meta, *operands)


def temporal_kernel(scale, shifts, meta, place, query_own, query_far, *rest):
    pairs, (out_own, out_far) = rest[:-2], rest[-2:]
    slots = len(pairs)
    half = query_own.shape[1]
    heads = meta.shape[0] // 3
    band = meta[2 * heads + pl.program_id(0)]
    side, pair_number, frames = place[0], place[1], place[2]
    size = PIXEL_BLOCK
    row = lax.broadcasted_iota(jnp.int32, (2 * size, slots * size), 0)
    column = lax.broadcasted_iota(jnp.int32, (2 * size, slots * size), 1)
    row_frame = 2 * pair_number + jnp.where(row >= size, 1 - side, side)
    slot = column // size
    column_frame = 2 * pair_number + jnp.where(slot % 2 == 1, 1 - side, side)
    shift = jnp.zeros_like(slot)
    for number, step in enumerate(shifts):
        shift = jnp.where(slot // 2 == number, step, shift)
    column_frame = column_frame + 2 * shift
    keep = (
        (row % size == column % size)
        & (jnp.abs(row_frame - column_frame) <= band)
        & (column_frame >= 0)
        & (column_frame < frames)
    )
    for start in range(0, half, size):
        part = slice(start, start + size)
        query = jnp.concatenate([query_own[0, part, :], query_far[0, part, :]], axis=0)
        key = jnp.concatenate([pair[0, 0, part, :] for pair in pairs], axis=0)
        value = jnp.concatenate([pair[1, 0, part, :] for pair in pairs], axis=0)
        scores = lax.dot_general(query, key, (((1,), (1,)), ((), ())), preferred_element_type=jnp.float32)
        scores = jnp.where(keep, scores, MASKED)
        peak = jnp.max(scores, axis=1, keepdims=True)
        weights = jnp.where(keep, jnp.exp2((scores - peak) * scale), 0.0)
        total = jnp.sum(weights, axis=1, keepdims=True)
        result = jnp.dot(weights.astype(jnp.bfloat16), value, preferred_element_type=jnp.float32) / total
        out_own[0, part, :] = result[:size].astype(jnp.bfloat16)
        out_far[0, part, :] = result[size:].astype(jnp.bfloat16)


def temporal(meta, place, shifts, query_own, query_far, pairs):
    half = query_own.shape[1]
    single = pl.BlockSpec((1, half, HEAD_DIM), lambda i, *_: (i, 0, 0))
    double = pl.BlockSpec((2, 1, half, HEAD_DIM), lambda i, *_: (0, i, 0, 0))
    out = jax.ShapeDtypeStruct(query_own.shape, jnp.bfloat16)
    return pl.pallas_call(
        functools.partial(temporal_kernel, math.log2(math.e) / math.sqrt(HEAD_DIM), shifts),
        out_shape=(out, out),
        grid_spec=pltpu.PrefetchScalarGridSpec(
            num_scalar_prefetch=2,
            grid=(TEMP_HEADS,),
            in_specs=[single, single] + [double] * len(pairs),
            out_specs=(single, single),
        ),
        compiler_params=pltpu.CompilerParams(vmem_limit_bytes=VMEM_BYTES),
        cost_estimate=pl.CostEstimate(
            flops=TEMP_HEADS * half * len(pairs) * PIXEL_BLOCK * HEAD_DIM * 8,
            bytes_accessed=TEMP_HEADS * half * HEAD_DIM * 2 * (4 + 2 * len(pairs)),
            transcendentals=TEMP_HEADS * half * 2 * len(pairs) * PIXEL_BLOCK,
        ),
        name="temporal_heads",
    )(meta, place, query_own, query_far, *pairs)


def finish_kernel(meta, place, own, far, so_far, out, sems):
    heads = meta.shape[0] // 3
    half = own.shape[1]
    side = place[0]
    for number in range(TEMP_HEADS):
        columns = pl.ds(pl.multiple_of(meta[heads + number] * HEAD_DIM, HEAD_DIM), HEAD_DIM)
        for rows_of, source, sem in ((side, own, 0), (1 - side, far, 1)):
            rows = pl.ds(pl.multiple_of(rows_of * half, half), half)
            pltpu.make_async_copy(source.at[number], out.at[rows, columns], sems.at[sem]).start()
    for sem, whole in enumerate((own, far)):
        pltpu.make_async_copy(whole, whole, sems.at[sem]).wait()


def finish(meta, place, own, far, so_far):
    any_spec = pl.BlockSpec(memory_space=pl.ANY)
    smem_spec = pl.BlockSpec(memory_space=pltpu.SMEM)
    return pl.pallas_call(
        finish_kernel,
        out_shape=jax.ShapeDtypeStruct(so_far.shape, so_far.dtype),
        in_specs=[smem_spec] * 2 + [any_spec] * 3,
        out_specs=any_spec,
        scratch_shapes=[pltpu.SemaphoreType.DMA((2,))],
        input_output_aliases={4: 0},
        cost_estimate=pl.CostEstimate(flops=0, bytes_accessed=4 * own.size * 2, transcendentals=0),
        name="finish",
    )(meta, place, own, far, so_far)


def shards(queries, keys, values, labels, band):
    count = lax.axis_size("frame")
    frames = count // 2
    index = lax.axis_index("frame").astype(jnp.int32)
    place = jnp.stack([(index // 2) % 2, index // 4, jnp.int32(frames)])
    reach = frames // 4

    keys_far = swap_bit(keys, 0)
    values_far = swap_bit(values, 0)
    meta, pair_keep, pair_send, query_keep, query_send = extract(place, labels, band, queries, keys, values)
    pair_got = swap_bit(pair_send, 1)
    query_got = swap_bit(query_send, 1)

    shifts, pairs = [0], [pair_keep, pair_got]
    below, above = [pair_keep, pair_got], [pair_keep, pair_got]
    for step in range(1, reach + 1):
        below = [shift_pairs(block, 1) for block in below]
        above = [shift_pairs(block, -1) for block in above]
        shifts += [-step, step]
        pairs += below + above

    heads = labels.shape[0]
    spatial_count = heads - TEMP_HEADS
    piece = spatial_count // SPATIAL_PIECES
    result = None
    for number in range(SPATIAL_PIECES):
        result = spatial_piece(meta, number * piece, piece, queries, keys, values, keys_far, values_far, result)

    out_keep, out_send = temporal(meta, place, tuple(shifts), query_keep, query_got, pairs)
    out_got = swap_bit(out_send, 1)
    return finish(meta, place, out_keep, out_got, result)


def solution(mesh):
    placed = (
        P(("group", "frame"), None),
        P(("group", "frame"), None),
        P(("group", "frame"), None),
        P("group"),
        P("group"),
    )
    return jax.shard_map(
        shards, mesh=mesh, in_specs=placed, out_specs=P(("group", "frame"), None), check_vma=False
    )
```

```python
import functools
import math

import jax
import jax.numpy as jnp
from jax import lax
from jax.experimental import pallas as pl
from jax.experimental.pallas import tpu as pltpu
from jax.sharding import PartitionSpec as P

TEMP_HEADS = 10
HEAD_DIM = 128
PIXEL_BLOCK = 32
SPATIAL_PIECES = (9, 9, 12)
STEP_HEADS = 3
HIGH = 5
LEVELS = (0, 1, 2, 3, 4, 5, 6, 8, 2 * (TEMP_HEADS - HIGH))
MASKED = -1e30
MIB = 1024 * 1024
HBM = pl.BlockSpec(memory_space=pltpu.HBM)
SMEM = pl.BlockSpec(memory_space=pltpu.SMEM)
VMEM = pl.BlockSpec(memory_space=pltpu.VMEM)


def swap_bit(block, bit):
    count = lax.axis_size("frame")
    return lax.ppermute(block, "frame", [(i, i ^ (1 << bit)) for i in range(count)])


def swap_pairs(block, first, distance):
    count = lax.axis_size("frame")
    places = count // 4
    route = []
    for low in range(first, places - 1, 2):
        if low - (distance - 1) >= 0:
            route += [(low * 4 + i, low * 4 + 4 + i) for i in range(4)]
        if low + distance < places:
            route += [(low * 4 + 4 + i, low * 4 + i) for i in range(4)]
    return lax.ppermute(block, "frame", route)


def largest(value):
    count = lax.axis_size("group")
    result = value
    for shift in range(1, count):
        route = [(i, (i + shift) % count) for i in range(count)]
        result = jnp.maximum(result, lax.ppermute(value, "group", route))
    return result


def position():
    index = lax.axis_index("frame")
    return (index // 2) % 2, index // 4


def columns_of(head):
    return pl.ds(pl.multiple_of(head * HEAD_DIM, HEAD_DIM), HEAD_DIM)


def rows_of(side, half):
    return pl.ds(pl.multiple_of(side * half, half), half)


def extract_kernel(
    reach, labels_hbm, band_hbm, queries, keys, values,
    meta, choice, pair_keep, high_send, low_send, query_keep, query_send, labels, band, found, sems,
):
    heads = labels.shape[0]
    half = query_keep.shape[1]
    side, _ = position()
    small = [
        pltpu.make_async_copy(labels_hbm, labels, sems.at[0]),
        pltpu.make_async_copy(band_hbm, band, sems.at[1]),
    ]
    for copy in small:
        copy.start()
    for copy in small:
        copy.wait()

    def one_head(head, counts):
        spatial, temporal = counts
        is_temporal = labels[head] == 1

        @pl.when(is_temporal)
        def _():
            found[temporal] = head

        @pl.when(jnp.logical_not(is_temporal))
        def _():
            meta[spatial] = head

        step = is_temporal.astype(jnp.int32)
        return spatial + 1 - step, temporal + step

    lax.fori_loop(0, heads, one_head, (jnp.int32(0), jnp.int32(0)))
    listed_heads = [found[number] for number in range(TEMP_HEADS)]
    bands = [band[head] for head in listed_heads]
    for number, head in enumerate(listed_heads):
        rank = jnp.int32(0)
        for other in range(TEMP_HEADS):
            if other != number:
                before = bands[other] >= bands[number] if other < number else bands[other] > bands[number]
                rank = rank + before.astype(jnp.int32)
        meta[heads + rank] = head
        meta[2 * heads + rank] = bands[number]

    def one_copy(rank, carry):
        columns = columns_of(meta[heads + rank])
        kept, sent = rows_of(side, half), rows_of(1 - side, half)
        pltpu.make_async_copy(queries.at[kept, columns], query_keep.at[rank], sems.at[2]).start()
        pltpu.make_async_copy(queries.at[sent, columns], query_send.at[rank], sems.at[3]).start()
        for number, source in enumerate((keys, values)):
            pltpu.make_async_copy(source.at[kept, columns], pair_keep.at[rank, number], sems.at[4]).start()

            @pl.when(rank < HIGH)
            def _():
                pltpu.make_async_copy(source.at[sent, columns], high_send.at[rank, number], sems.at[5]).start()

            @pl.when(rank >= HIGH)
            def _():
                pltpu.make_async_copy(source.at[sent, columns], low_send.at[rank - HIGH, number], sems.at[6]).start()

        return carry

    lax.fori_loop(0, TEMP_HEADS, one_copy, jnp.int32(0))

    items = 3 * heads
    places = items + 2 * TEMP_HEADS
    for number in range(2 * TEMP_HEADS):
        meta[items + number] = 0
    listed = jnp.int32(0)
    for number in range(TEMP_HEADS - HIGH):
        for kind in range(2):
            is_needed = meta[2 * heads + HIGH + number] >= 2 * reach - 1 + kind
            meta[places + 2 * number + kind] = listed

            @pl.when(is_needed)
            def _():
                meta[items + listed] = 2 * number + kind

            listed = listed + is_needed.astype(jnp.int32)
    choice[0] = sum((listed > level).astype(jnp.int32) for level in LEVELS[:-1])
    for number, whole in enumerate((query_keep, query_send, pair_keep, high_send, low_send)):
        pltpu.make_async_copy(whole, whole, sems.at[2 + number]).wait()


def extract(reach, labels, band, queries, keys, values):
    rows = queries.shape[0]
    half = rows // 2
    single = jax.ShapeDtypeStruct((TEMP_HEADS, half, HEAD_DIM), jnp.bfloat16)
    pair = [
        jax.ShapeDtypeStruct((count, 2, half, HEAD_DIM), jnp.bfloat16)
        for count in (TEMP_HEADS, HIGH, TEMP_HEADS - HIGH)
    ]
    return pl.pallas_call(
        functools.partial(extract_kernel, reach),
        out_shape=(
            jax.ShapeDtypeStruct((3 * labels.shape[0] + 4 * TEMP_HEADS,), jnp.int32),
            jax.ShapeDtypeStruct((1,), jnp.int32),
            *pair, single, single,
        ),
        in_specs=[HBM] * 5,
        out_specs=(SMEM, SMEM) + (VMEM,) * 5,
        scratch_shapes=[
            pltpu.SMEM(labels.shape, jnp.int32),
            pltpu.SMEM(band.shape, jnp.int32),
            pltpu.SMEM((TEMP_HEADS,), jnp.int32),
            pltpu.SemaphoreType.DMA((7,)),
        ],
        compiler_params=pltpu.CompilerParams(vmem_limit_bytes=58 * MIB),
        cost_estimate=pl.CostEstimate(flops=0, bytes_accessed=12 * TEMP_HEADS * half * HEAD_DIM * 2, transcendentals=0),
        name="extract_temporal",
    )(labels, band, queries, keys, values)


def spatial_kernel(scale, first, meta, *refs):
    heads = [refs[5 * number : 5 * number + 5] for number in range(STEP_HEADS)]
    out, key_all, value_all, held, sems = refs[-5:]
    step, steps = pl.program_id(0), pl.num_programs(0)
    slot = step % 2
    rows = held.shape[2]
    half = rows // 2

    def store(step, slot, number):
        columns = columns_of(meta[first + step * STEP_HEADS + number])
        return pltpu.make_async_copy(held.at[slot, number], out.at[:, columns], sems.at[slot, number])

    @pl.when(step >= 2)
    def _():
        for number in range(STEP_HEADS):
            store(step - 2, slot, number).wait()

    for number, (_, key_own, value_own, key_far, value_far) in enumerate(heads):
        key_all[number, :rows, :] = key_own[...]
        key_all[number, rows:, :] = key_far[...]
        value_all[number, :rows, :HEAD_DIM] = value_own[...]
        value_all[number, rows:, :HEAD_DIM] = value_far[...]
        value_all[number, :, HEAD_DIM:] = jnp.ones((2 * rows, HEAD_DIM), jnp.bfloat16)
    parts = [(number, slice(start, start + half)) for number in range(STEP_HEADS) for start in (0, half)]
    scores = [
        lax.dot_general(
            heads[number][0][part, :], key_all[number], (((1,), (1,)), ((), ())), preferred_element_type=jnp.float32
        )
        for number, part in parts
    ]
    for (number, part), score in zip(parts, scores):
        peak = jnp.max(score, axis=1, keepdims=True)
        weights = jnp.exp2((score - peak) * scale).astype(jnp.bfloat16)
        both = jnp.dot(weights, value_all[number], preferred_element_type=jnp.float32)
        held[slot, number, part, :] = (both[:, :HEAD_DIM] / both[:, HEAD_DIM:]).astype(jnp.bfloat16)
    for number in range(STEP_HEADS):
        store(step, slot, number).start()

    @pl.when(step == steps - 1)
    def _():
        for number in range(STEP_HEADS):
            store(step, slot, number).wait()

    @pl.when((step == steps - 1) & (steps >= 2))
    def _():
        for number in range(STEP_HEADS):
            store(step - 1, 1 - slot, number).wait()


def spatial_piece(meta, first, count, queries, keys, values, keys_far, values_far, so_far):
    rows = queries.shape[0]
    operands, specs = [], []
    for number in range(STEP_HEADS):
        place = lambda i, meta, number=number: (0, meta[first + i * STEP_HEADS + number])
        operands += [queries, keys, values, keys_far, values_far]
        specs += [pl.BlockSpec((rows, HEAD_DIM), place)] * 5
    aliases = {}
    if so_far is not None:
        operands.append(so_far)
        specs.append(HBM)
        aliases = {len(operands): 0}
    return pl.pallas_call(
        functools.partial(spatial_kernel, math.log2(math.e) / math.sqrt(HEAD_DIM), first),
        out_shape=jax.ShapeDtypeStruct(queries.shape, jnp.bfloat16),
        grid_spec=pltpu.PrefetchScalarGridSpec(
            num_scalar_prefetch=1,
            grid=(count // STEP_HEADS,),
            in_specs=specs,
            out_specs=HBM,
            scratch_shapes=[
                pltpu.VMEM((STEP_HEADS, 2 * rows, HEAD_DIM), jnp.bfloat16),
                pltpu.VMEM((STEP_HEADS, 2 * rows, 2 * HEAD_DIM), jnp.bfloat16),
                pltpu.VMEM((2, STEP_HEADS, rows, HEAD_DIM), jnp.bfloat16),
                pltpu.SemaphoreType.DMA((2, STEP_HEADS)),
            ],
        ),
        input_output_aliases=aliases,
        compiler_params=pltpu.CompilerParams(vmem_limit_bytes=50 * MIB),
        cost_estimate=pl.CostEstimate(
            flops=count * rows * 2 * rows * HEAD_DIM * 4,
            bytes_accessed=count * 6 * rows * HEAD_DIM * 2,
            transcendentals=count * rows * 2 * rows,
        ),
        name="spatial_heads",
    )(meta, *operands)


def pack_kernel(reach, meta, own_a, low_a, own_b, low_b, for_a, for_b, sems):
    heads = (meta.shape[0] - 4 * TEMP_HEADS) // 3
    side, place = position()
    even = place % 2 == 0
    sources = (
        (jnp.where(even, place + reach - 1, place - reach + 1), own_a, low_a, for_b, sems.at[0]),
        (jnp.where(even, place - reach + 1, place + reach - 1), own_b, low_b, for_a, sems.at[1]),
    )

    def one_item(number, carry):
        item = meta[3 * heads + number]
        head, kind = item // 2, item % 2
        for origin, own, low, out, sem in sources:
            near = (origin < reach).astype(jnp.int32)
            is_own = (near + kind + side) % 2 == 0

            @pl.when(is_own)
            def _():
                pltpu.make_async_copy(own.at[HIGH + head], out.at[number], sem).start()

            @pl.when(jnp.logical_not(is_own))
            def _():
                pltpu.make_async_copy(low.at[head], out.at[number], sem).start()

        return carry

    lax.fori_loop(0, for_a.shape[0], one_item, jnp.int32(0))
    pltpu.make_async_copy(for_a, for_a, sems.at[1]).wait()
    pltpu.make_async_copy(for_b, for_b, sems.at[0]).wait()


def pack(meta, reach, size, own, low):
    out = jax.ShapeDtypeStruct((size,) + low[0].shape[1:], jnp.bfloat16)
    return pl.pallas_call(
        functools.partial(pack_kernel, reach),
        out_shape=(out, out),
        in_specs=[SMEM] + [HBM] * 4,
        out_specs=(VMEM, VMEM),
        scratch_shapes=[pltpu.SemaphoreType.DMA((2,))],
        compiler_params=pltpu.CompilerParams(vmem_limit_bytes=12 * MIB),
        name="pack_items",
    )(meta, own[0], low[0], own[1], low[1])


def temporal_kernel(scale, frames, reach, is_high, meta, query_own, query_far, *rest):
    refs, (out_own, out_far) = rest[:-2], rest[-2:]
    count, half = out_far.shape[:2]
    heads = (meta.shape[0] - 4 * TEMP_HEADS) // 3
    first_head = 0 if is_high else HIGH
    side, place = position()
    odd = place % 2 == 1
    size = PIXEL_BLOCK

    shifts = [jnp.int32(0)]
    for distance in range(1, reach):
        up = jnp.where(odd, -distance, distance)
        shifts += [up, -up]
    pairs, last = refs[: 2 * len(shifts)], refs[2 * len(shifts) :]
    lower = place < reach
    from_a = lower != odd
    if last:
        shifts.append(jnp.where(lower, reach, -reach))
    slots = 2 * len(shifts)
    row = lax.broadcasted_iota(jnp.int32, (2 * size, 1), 0)
    column = lax.broadcasted_iota(jnp.int32, (1, slots * size), 1)
    row_frame = jnp.where(row >= size, 1 - side, side) + 2 * place
    slot = column // size
    shift = jnp.zeros_like(slot)
    for number, step in enumerate(shifts):
        shift = jnp.where(slot // 2 == number, step, shift)
    first_of = side
    if last and not is_high:
        first_of = jnp.where(slot // 2 == len(shifts) - 1, jnp.where(lower, 0, 1), side)
    column_frame = jnp.where(slot % 2 == 1, 1 - first_of, first_of) + 2 * (place + shift)
    far = 4 * frames
    column_frame = jnp.where((column_frame >= 0) & (column_frame < frames), column_frame, far)
    apart = jnp.where(row % size == column % size, jnp.abs(row_frame - column_frame), far)
    parts = [slice(start, start + size) for start in range(0, half, size)]

    def one_head(number, carry):
        head = first_head + number
        keep = apart <= meta[2 * heads + head]

        def stacked(kind, part):
            blocks = [pair[head if pair.shape[0] == TEMP_HEADS else number, kind, part, :] for pair in pairs]
            if is_high:
                for by_a, by_b in (last[:2], last[2:]):
                    blocks.append(jnp.where(from_a, by_a[number, kind, part, :], by_b[number, kind, part, :]))
            elif last:
                for which in range(2):
                    item = meta[3 * heads + 2 * TEMP_HEADS + 2 * number + which]
                    item = jnp.minimum(item, last[0].shape[0] - 1)
                    by_a, by_b = (block[item, kind, part, :] for block in last)
                    blocks.append(jnp.where(from_a, by_a, by_b))
            return jnp.concatenate(blocks, axis=0)

        scores = []
        for part in parts:
            query = jnp.concatenate([query_own[head, part, :], query_far[head, part, :]], axis=0)
            score = lax.dot_general(
                query, stacked(0, part), (((1,), (1,)), ((), ())), preferred_element_type=jnp.float32
            )
            scores.append(jnp.where(keep, score, MASKED))
        weights = []
        for score in scores:
            peak = jnp.max(score, axis=1, keepdims=True)
            weight = jnp.exp2((score - peak) * scale)
            weights.append((weight.astype(jnp.bfloat16), jnp.sum(weight, axis=1, keepdims=True)))
        results = [
            jnp.dot(weight, stacked(1, part), preferred_element_type=jnp.float32) / total
            for part, (weight, total) in zip(parts, weights)
        ]
        for part, result in zip(parts, results):
            out_own[number, part, :] = result[:size].astype(jnp.bfloat16)
            out_far[number, part, :] = result[size:].astype(jnp.bfloat16)
        return carry

    lax.fori_loop(0, count, one_head, jnp.int32(0), unroll=count)


def temporal(meta, frames, reach, is_high, query_own, query_far, pairs, last):
    half = query_own.shape[1]
    count = HIGH if is_high else TEMP_HEADS - HIGH
    operands = [meta, query_own, query_far, *pairs, *last]
    out = jax.ShapeDtypeStruct((count, half, HEAD_DIM), jnp.bfloat16)
    slots = 2 + len(pairs)
    return pl.pallas_call(
        functools.partial(temporal_kernel, math.log2(math.e) / math.sqrt(HEAD_DIM), frames, reach, is_high),
        out_shape=(out, out),
        in_specs=[SMEM] + [VMEM] * (len(operands) - 1),
        out_specs=(VMEM, VMEM),
        compiler_params=pltpu.CompilerParams(vmem_limit_bytes=44 * MIB),
        cost_estimate=pl.CostEstimate(
            flops=count * half * slots * PIXEL_BLOCK * HEAD_DIM * 8,
            bytes_accessed=count * half * HEAD_DIM * 2 * (4 + 2 * slots),
            transcendentals=count * half * 2 * slots * PIXEL_BLOCK,
        ),
        name="temporal_heads",
    )(*operands)


def finish_kernel(meta, *refs):
    blocks, (_, out, sems) = refs[:-3], refs[-3:]
    heads = (meta.shape[0] - 4 * TEMP_HEADS) // 3
    side, _ = position()
    for turn, first in ((0, 0), (1, 1)):
        head = 0
        for block in blocks[first::2]:
            count, half = block.shape[:2]
            rows = rows_of(side if turn == 0 else 1 - side, half)
            for number in range(count):
                columns = columns_of(meta[heads + head])
                pltpu.make_async_copy(block.at[number], out.at[rows, columns], sems.at[0]).start()
                head += 1
    for block in blocks:
        pltpu.make_async_copy(block, block, sems.at[0]).wait()


def finish(meta, blocks, so_far):
    return pl.pallas_call(
        finish_kernel,
        out_shape=jax.ShapeDtypeStruct(so_far.shape, so_far.dtype),
        in_specs=[SMEM] + [VMEM] * len(blocks) + [HBM],
        out_specs=HBM,
        scratch_shapes=[pltpu.SemaphoreType.DMA((1,))],
        input_output_aliases={1 + len(blocks): 0},
        compiler_params=pltpu.CompilerParams(vmem_limit_bytes=4 * MIB),
        cost_estimate=pl.CostEstimate(flops=0, bytes_accessed=4 * so_far.size // 4, transcendentals=0),
        name="finish",
    )(meta, *blocks, so_far)


def shards(queries, keys, values, labels, band):
    frames = lax.axis_size("frame") // 2
    reach = frames // 4

    keys_far = swap_bit(keys, 0)
    values_far = swap_bit(values, 0)
    meta, choice, pair_keep, high_send, low_send, query_keep, query_send = extract(
        reach, labels, band, queries, keys, values
    )

    def attend_piece(result, number):
        first, count = sum(SPATIAL_PIECES[:number]), SPATIAL_PIECES[number]
        return spatial_piece(meta, first, count, queries, keys, values, keys_far, values_far, result)

    def both_swaps(held, distance):
        return swap_pairs(held[1], 0, distance), swap_pairs(held[0], 1, distance)

    own = both_swaps((pair_keep, pair_keep), 1)
    high_got = swap_bit(high_send, 1)
    low_got = swap_bit(low_send, 1)
    result = attend_piece(None, 0)
    high_got, result = lax.optimization_barrier((high_got, result))
    high = both_swaps((high_got, high_got), 1)
    result = attend_piece(result, 1)
    own, low_got, query_send, choice, result = lax.optimization_barrier((own, low_got, query_send, choice, result))
    low = both_swaps((low_got, low_got), 1)
    high_pairs = [pair_keep, high_got, own[0], high[0], own[1], high[1]]
    low_pairs = [pair_keep, low_got, own[0], low[0], own[1], low[1]]
    for distance in range(2, reach):
        own, high, low = (both_swaps(held, distance) for held in (own, high, low))
        high_pairs += [own[0], high[0], own[1], high[1]]
        low_pairs += [own[0], low[0], own[1], low[1]]
    own_last = both_swaps((own[0][:HIGH], own[1][:HIGH]), reach)
    high, result = lax.optimization_barrier((high, result))
    choice = largest(choice)
    query_got = swap_bit(query_send, 1)
    result = attend_piece(result, 2)
    own, high, low, own_last, query_got, choice, result = lax.optimization_barrier(
        (own, high, low, own_last, query_got, choice, result)
    )

    def last_swaps(size, meta, own, high, low, own_last, query_keep, query_got, high_pairs, low_pairs):
        high_last = both_swaps(high, reach)
        items = []
        if size:
            for_a, for_b = pack(meta, reach, size, own, low)
            items = [swap_pairs(for_a, 0, reach), swap_pairs(for_b, 1, reach)]
        else:
            keep_low, send_low = temporal(meta, frames, reach, False, query_keep, query_got, low_pairs, items)
            query_keep, send_low = lax.optimization_barrier((query_keep, send_low))
        keep_high, send_high = temporal(
            meta, frames, reach, True, query_keep, query_got, high_pairs, [*own_last, *high_last]
        )
        if size:
            query_keep, send_high = lax.optimization_barrier((query_keep, send_high))
            keep_low, send_low = temporal(meta, frames, reach, False, query_keep, query_got, low_pairs, items)
        return keep_high, swap_bit(send_high, 1), keep_low, swap_bit(send_low, 1)

    blocks = lax.switch(
        choice[0], [functools.partial(last_swaps, size) for size in LEVELS],
        meta, own, high, low, own_last, query_keep, query_got, high_pairs, low_pairs,
    )
    return finish(meta, blocks, result)


def solution(mesh):
    placed = (
        P(("group", "frame"), None),
        P(("group", "frame"), None),
        P(("group", "frame"), None),
        P("group"),
        P("group"),
    )
    return jax.shard_map(
        shards, mesh=mesh, in_specs=placed, out_specs=P(("group", "frame"), None), check_vma=False
    )
```

```python
import functools
import math

import jax
import jax.numpy as jnp
from jax import lax
from jax.experimental import pallas as pl
from jax.experimental.pallas import tpu as pltpu
from jax.sharding import PartitionSpec as P

TEMP_HEADS = 10
HEAD_DIM = 128
PIXEL_BLOCK = 32
SPATIAL_PIECES = (9, 9, 12)
STEP_HEADS = 3
HIGH = 5
LEVELS = (0, 2, 3, 4, 5, 6, 2 * (TEMP_HEADS - HIGH))
MASKED = -1e30
MIB = 1024 * 1024
HBM = pl.BlockSpec(memory_space=pltpu.HBM)
SMEM = pl.BlockSpec(memory_space=pltpu.SMEM)
VMEM = pl.BlockSpec(memory_space=pltpu.VMEM)


def swap_bit(block, bit):
    count = lax.axis_size("frame")
    return lax.ppermute(block, "frame", [(i, i ^ (1 << bit)) for i in range(count)])


def swap_pairs(block, first, distance):
    count = lax.axis_size("frame")
    places = count // 4
    route = []
    for low in range(first, places - 1, 2):
        if low - (distance - 1) >= 0:
            route += [(low * 4 + i, low * 4 + 4 + i) for i in range(4)]
        if low + distance < places:
            route += [(low * 4 + 4 + i, low * 4 + i) for i in range(4)]
    return lax.ppermute(block, "frame", route)


def largest(value):
    count = lax.axis_size("group")
    result = value
    for shift in range(1, count):
        route = [(i, (i + shift) % count) for i in range(count)]
        result = jnp.maximum(result, lax.ppermute(value, "group", route))
    return result


def position():
    index = lax.axis_index("frame")
    return (index // 2) % 2, index // 4


def columns_of(head):
    return pl.ds(pl.multiple_of(head * HEAD_DIM, HEAD_DIM), HEAD_DIM)


def rows_of(side, half):
    return pl.ds(pl.multiple_of(side * half, half), half)


def extract_kernel(
    reach, labels_hbm, band_hbm, queries, keys, values,
    meta, choice, pair_keep, high_send, low_send, query_keep, query_send, labels, band, found, sems,
):
    heads = labels.shape[0]
    half = query_keep.shape[1]
    side, _ = position()
    small = [
        pltpu.make_async_copy(labels_hbm, labels, sems.at[0]),
        pltpu.make_async_copy(band_hbm, band, sems.at[1]),
    ]
    for copy in small:
        copy.start()
    for copy in small:
        copy.wait()

    def one_head(head, counts):
        spatial, temporal = counts
        is_temporal = labels[head] == 1

        @pl.when(is_temporal)
        def _():
            found[temporal] = head

        @pl.when(jnp.logical_not(is_temporal))
        def _():
            meta[spatial] = head

        step = is_temporal.astype(jnp.int32)
        return spatial + 1 - step, temporal + step

    lax.fori_loop(0, heads, one_head, (jnp.int32(0), jnp.int32(0)))
    listed_heads = [found[number] for number in range(TEMP_HEADS)]
    bands = [band[head] for head in listed_heads]
    for number, head in enumerate(listed_heads):
        rank = jnp.int32(0)
        for other in range(TEMP_HEADS):
            if other != number:
                before = bands[other] >= bands[number] if other < number else bands[other] > bands[number]
                rank = rank + before.astype(jnp.int32)
        meta[heads + rank] = head
        meta[2 * heads + rank] = bands[number]

    def one_copy(rank, carry):
        columns = columns_of(meta[heads + rank])
        kept, sent = rows_of(side, half), rows_of(1 - side, half)
        pltpu.make_async_copy(queries.at[kept, columns], query_keep.at[rank], sems.at[2]).start()
        pltpu.make_async_copy(queries.at[sent, columns], query_send.at[rank], sems.at[3]).start()
        for number, source in enumerate((keys, values)):
            pltpu.make_async_copy(source.at[kept, columns], pair_keep.at[rank, number], sems.at[4]).start()

            @pl.when(rank < HIGH)
            def _():
                pltpu.make_async_copy(source.at[sent, columns], high_send.at[rank, number], sems.at[5]).start()

            @pl.when(rank >= HIGH)
            def _():
                pltpu.make_async_copy(source.at[sent, columns], low_send.at[rank - HIGH, number], sems.at[6]).start()

        return carry

    lax.fori_loop(0, TEMP_HEADS, one_copy, jnp.int32(0))

    items = 3 * heads
    places = items + 2 * TEMP_HEADS
    for number in range(2 * TEMP_HEADS):
        meta[items + number] = 0
    listed = jnp.int32(0)
    for number in range(TEMP_HEADS - HIGH):
        for kind in range(2):
            is_needed = meta[2 * heads + HIGH + number] >= 2 * reach - 1 + kind
            meta[places + 2 * number + kind] = listed

            @pl.when(is_needed)
            def _():
                meta[items + listed] = 2 * number + kind

            listed = listed + is_needed.astype(jnp.int32)
    choice[0] = sum((listed > level).astype(jnp.int32) for level in LEVELS[:-1])
    for number, whole in enumerate((query_keep, query_send, pair_keep, high_send, low_send)):
        pltpu.make_async_copy(whole, whole, sems.at[2 + number]).wait()


def extract(reach, labels, band, queries, keys, values):
    rows = queries.shape[0]
    half = rows // 2
    single = jax.ShapeDtypeStruct((TEMP_HEADS, half, HEAD_DIM), jnp.bfloat16)
    pair = [
        jax.ShapeDtypeStruct((count, 2, half, HEAD_DIM), jnp.bfloat16)
        for count in (TEMP_HEADS, HIGH, TEMP_HEADS - HIGH)
    ]
    return pl.pallas_call(
        functools.partial(extract_kernel, reach),
        out_shape=(
            jax.ShapeDtypeStruct((3 * labels.shape[0] + 4 * TEMP_HEADS,), jnp.int32),
            jax.ShapeDtypeStruct((1,), jnp.int32),
            *pair, single, single,
        ),
        in_specs=[HBM] * 5,
        out_specs=(SMEM, SMEM) + (VMEM,) * 5,
        scratch_shapes=[
            pltpu.SMEM(labels.shape, jnp.int32),
            pltpu.SMEM(band.shape, jnp.int32),
            pltpu.SMEM((TEMP_HEADS,), jnp.int32),
            pltpu.SemaphoreType.DMA((7,)),
        ],
        compiler_params=pltpu.CompilerParams(vmem_limit_bytes=58 * MIB),
        cost_estimate=pl.CostEstimate(flops=0, bytes_accessed=12 * TEMP_HEADS * half * HEAD_DIM * 2, transcendentals=0),
        name="extract_temporal",
    )(labels, band, queries, keys, values)


def spatial_kernel(scale, first, meta, *refs):
    heads = [refs[5 * number : 5 * number + 5] for number in range(STEP_HEADS)]
    out, key_all, value_all, held, sems = refs[-5:]
    step, steps = pl.program_id(0), pl.num_programs(0)
    slot = step % 2
    rows = held.shape[2]
    half = rows // 2

    def store(step, slot, number):
        columns = columns_of(meta[first + step * STEP_HEADS + number])
        return pltpu.make_async_copy(held.at[slot, number], out.at[:, columns], sems.at[slot, number])

    @pl.when(step >= 2)
    def _():
        for number in range(STEP_HEADS):
            store(step - 2, slot, number).wait()

    for number, (_, key_own, value_own, key_far, value_far) in enumerate(heads):
        key_all[number, :rows, :] = key_own[...]
        key_all[number, rows:, :] = key_far[...]
        value_all[number, :rows, :HEAD_DIM] = value_own[...]
        value_all[number, rows:, :HEAD_DIM] = value_far[...]
        value_all[number, :, HEAD_DIM:] = jnp.ones((2 * rows, HEAD_DIM), jnp.bfloat16)
    parts = [(number, slice(start, start + half)) for number in range(STEP_HEADS) for start in (0, half)]
    scores = [
        lax.dot_general(
            heads[number][0][part, :], key_all[number], (((1,), (1,)), ((), ())), preferred_element_type=jnp.float32
        )
        for number, part in parts
    ]
    for (number, part), score in zip(parts, scores):
        peak = jnp.max(score, axis=1, keepdims=True)
        weights = jnp.exp2((score - peak) * scale).astype(jnp.bfloat16)
        both = jnp.dot(weights, value_all[number], preferred_element_type=jnp.float32)
        held[slot, number, part, :] = (both[:, :HEAD_DIM] / both[:, HEAD_DIM:]).astype(jnp.bfloat16)
    for number in range(STEP_HEADS):
        store(step, slot, number).start()

    @pl.when(step == steps - 1)
    def _():
        for number in range(STEP_HEADS):
            store(step, slot, number).wait()

    @pl.when((step == steps - 1) & (steps >= 2))
    def _():
        for number in range(STEP_HEADS):
            store(step - 1, 1 - slot, number).wait()


def spatial_piece(meta, first, count, queries, keys, values, keys_far, values_far, so_far):
    rows = queries.shape[0]
    operands, specs = [], []
    for number in range(STEP_HEADS):
        place = lambda i, meta, number=number: (0, meta[first + i * STEP_HEADS + number])
        operands += [queries, keys, values, keys_far, values_far]
        specs += [pl.BlockSpec((rows, HEAD_DIM), place)] * 5
    aliases = {}
    if so_far is not None:
        operands.append(so_far)
        specs.append(HBM)
        aliases = {len(operands): 0}
    return pl.pallas_call(
        functools.partial(spatial_kernel, math.log2(math.e) / math.sqrt(HEAD_DIM), first),
        out_shape=jax.ShapeDtypeStruct(queries.shape, jnp.bfloat16),
        grid_spec=pltpu.PrefetchScalarGridSpec(
            num_scalar_prefetch=1,
            grid=(count // STEP_HEADS,),
            in_specs=specs,
            out_specs=HBM,
            scratch_shapes=[
                pltpu.VMEM((STEP_HEADS, 2 * rows, HEAD_DIM), jnp.bfloat16),
                pltpu.VMEM((STEP_HEADS, 2 * rows, 2 * HEAD_DIM), jnp.bfloat16),
                pltpu.VMEM((2, STEP_HEADS, rows, HEAD_DIM), jnp.bfloat16),
                pltpu.SemaphoreType.DMA((2, STEP_HEADS)),
            ],
        ),
        input_output_aliases=aliases,
        compiler_params=pltpu.CompilerParams(vmem_limit_bytes=50 * MIB),
        cost_estimate=pl.CostEstimate(
            flops=count * rows * 2 * rows * HEAD_DIM * 4,
            bytes_accessed=count * 6 * rows * HEAD_DIM * 2,
            transcendentals=count * rows * 2 * rows,
        ),
        name="spatial_heads",
    )(meta, *operands)


def pack_kernel(reach, meta, own_a, low_a, own_b, low_b, for_a, for_b, sems):
    heads = (meta.shape[0] - 4 * TEMP_HEADS) // 3
    side, place = position()
    even = place % 2 == 0
    sources = (
        (jnp.where(even, place + reach - 1, place - reach + 1), own_a, low_a, for_b, sems.at[0]),
        (jnp.where(even, place - reach + 1, place + reach - 1), own_b, low_b, for_a, sems.at[1]),
    )

    def one_item(number, carry):
        item = meta[3 * heads + number]
        head, kind = item // 2, item % 2
        for origin, own, low, out, sem in sources:
            near = (origin < reach).astype(jnp.int32)
            is_own = (near + kind + side) % 2 == 0

            @pl.when(is_own)
            def _():
                pltpu.make_async_copy(own.at[HIGH + head], out.at[number], sem).start()

            @pl.when(jnp.logical_not(is_own))
            def _():
                pltpu.make_async_copy(low.at[head], out.at[number], sem).start()

        return carry

    lax.fori_loop(0, for_a.shape[0], one_item, jnp.int32(0))
    pltpu.make_async_copy(for_a, for_a, sems.at[1]).wait()
    pltpu.make_async_copy(for_b, for_b, sems.at[0]).wait()


def pack(meta, reach, size, own, low):
    out = jax.ShapeDtypeStruct((size,) + low[0].shape[1:], jnp.bfloat16)
    return pl.pallas_call(
        functools.partial(pack_kernel, reach),
        out_shape=(out, out),
        in_specs=[SMEM] + [HBM] * 4,
        out_specs=(VMEM, VMEM),
        scratch_shapes=[pltpu.SemaphoreType.DMA((2,))],
        compiler_params=pltpu.CompilerParams(vmem_limit_bytes=12 * MIB),
        name="pack_items",
    )(meta, own[0], low[0], own[1], low[1])


def temporal_kernel(scale, frames, reach, first_head, returned_head, meta, query_own, query_far, *rest):
    refs, (_, out, out_far, out_own, sems) = rest[:-5], rest[-5:]
    count, half = out_far.shape[:2]
    is_high = first_head < HIGH
    heads = (meta.shape[0] - 4 * TEMP_HEADS) // 3
    first_listed = 0 if is_high else HIGH
    side, place = position()
    odd = place % 2 == 1
    size = PIXEL_BLOCK

    shifts = [jnp.int32(0)]
    for distance in range(1, reach):
        up = jnp.where(odd, -distance, distance)
        shifts += [up, -up]
    pairs, last = refs[: 2 * len(shifts)], refs[2 * len(shifts) :]
    if returned_head is not None:
        last, returned = last[:-1], last[-1]
        for number in range(returned.shape[0]):
            columns = columns_of(meta[heads + returned_head + number])
            pltpu.make_async_copy(returned.at[number], out.at[rows_of(1 - side, half), columns], sems.at[1]).start()
    lower = place < reach
    from_a = lower != odd
    if last:
        shifts.append(jnp.where(lower, reach, -reach))
    slots = 2 * len(shifts)
    row = lax.broadcasted_iota(jnp.int32, (2 * size, 1), 0)
    column = lax.broadcasted_iota(jnp.int32, (1, slots * size), 1)
    row_frame = jnp.where(row >= size, 1 - side, side) + 2 * place
    slot = column // size
    shift = jnp.zeros_like(slot)
    for number, step in enumerate(shifts):
        shift = jnp.where(slot // 2 == number, step, shift)
    first_of = side
    if last and not is_high:
        first_of = jnp.where(slot // 2 == len(shifts) - 1, jnp.where(lower, 0, 1), side)
    column_frame = jnp.where(slot % 2 == 1, 1 - first_of, first_of) + 2 * (place + shift)
    far = 4 * frames
    column_frame = jnp.where((column_frame >= 0) & (column_frame < frames), column_frame, far)
    apart = jnp.where(row % size == column % size, jnp.abs(row_frame - column_frame), far)
    parts = [slice(start, start + size) for start in range(0, half, size)]

    def one_head(number, carry):
        head = first_head + number
        keep = apart <= meta[2 * heads + head]

        def stacked(kind, part):
            blocks = [pair[head if pair.shape[0] == TEMP_HEADS else head - first_listed, kind, part, :] for pair in pairs]
            if is_high:
                for by_a, by_b in (last[:2], last[2:]):
                    blocks.append(jnp.where(from_a, by_a[head, kind, part, :], by_b[head, kind, part, :]))
            elif last:
                for which in range(2):
                    item = meta[3 * heads + 2 * TEMP_HEADS + 2 * (head - HIGH) + which]
                    item = jnp.minimum(item, last[0].shape[0] - 1)
                    by_a, by_b = (block[item, kind, part, :] for block in last)
                    blocks.append(jnp.where(from_a, by_a, by_b))
            return jnp.concatenate(blocks, axis=0)

        scores = []
        for part in parts:
            query = jnp.concatenate([query_own[head, part, :], query_far[head, part, :]], axis=0)
            score = lax.dot_general(
                query, stacked(0, part), (((1,), (1,)), ((), ())), preferred_element_type=jnp.float32
            )
            scores.append(jnp.where(keep, score, MASKED))
        weights = []
        for score in scores:
            peak = jnp.max(score, axis=1, keepdims=True)
            weight = jnp.exp2((score - peak) * scale)
            weights.append((weight.astype(jnp.bfloat16), jnp.sum(weight, axis=1, keepdims=True)))
        results = [
            jnp.dot(weight, stacked(1, part), preferred_element_type=jnp.float32) / total
            for part, (weight, total) in zip(parts, weights)
        ]
        for part, result in zip(parts, results):
            out_own[number, part, :] = result[:size].astype(jnp.bfloat16)
            out_far[number, part, :] = result[size:].astype(jnp.bfloat16)
        columns = columns_of(meta[heads + head])
        pltpu.make_async_copy(out_own.at[number], out.at[rows_of(side, half), columns], sems.at[0]).start()
        return carry

    lax.fori_loop(0, count, one_head, jnp.int32(0))
    pltpu.make_async_copy(out_own, out_own, sems.at[0]).wait()
    if returned_head is not None:
        pltpu.make_async_copy(returned, returned, sems.at[1]).wait()


def temporal(meta, frames, reach, heads, query_own, query_far, pairs, last, so_far, returned=None):
    first_head, end = heads
    count, half = end - first_head, query_own.shape[1]
    operands = [meta, query_own, query_far, *pairs, *last]
    returned_head = None
    if returned is not None:
        returned_head, block = returned
        operands.append(block)
    specs = [SMEM] + [VMEM] * (len(operands) - 1) + [HBM]
    operands.append(so_far)
    slots = 2 + len(pairs)
    return pl.pallas_call(
        functools.partial(
            temporal_kernel, math.log2(math.e) / math.sqrt(HEAD_DIM), frames, reach, first_head, returned_head
        ),
        out_shape=(
            jax.ShapeDtypeStruct(so_far.shape, so_far.dtype),
            jax.ShapeDtypeStruct((count, half, HEAD_DIM), jnp.bfloat16),
        ),
        in_specs=specs,
        out_specs=(HBM, VMEM),
        scratch_shapes=[pltpu.VMEM((count, half, HEAD_DIM), jnp.bfloat16), pltpu.SemaphoreType.DMA((2,))],
        input_output_aliases={len(operands) - 1: 0},
        compiler_params=pltpu.CompilerParams(vmem_limit_bytes=44 * MIB),
        cost_estimate=pl.CostEstimate(
            flops=count * half * slots * PIXEL_BLOCK * HEAD_DIM * 8,
            bytes_accessed=count * half * HEAD_DIM * 2 * (4 + 2 * slots),
            transcendentals=count * half * 2 * slots * PIXEL_BLOCK,
        ),
        name="temporal_heads",
    )(*operands)


def finish_kernel(first_head, meta, *refs):
    blocks, (_, out, sem) = refs[:-3], refs[-3:]
    heads = (meta.shape[0] - 4 * TEMP_HEADS) // 3
    side, _ = position()
    head = first_head
    for block in blocks:
        count, half = block.shape[:2]
        for number in range(count):
            columns = columns_of(meta[heads + head])
            pltpu.make_async_copy(block.at[number], out.at[rows_of(1 - side, half), columns], sem).start()
            head += 1
    for block in blocks:
        pltpu.make_async_copy(block, block, sem).wait()


def finish(meta, first_head, blocks, so_far):
    return pl.pallas_call(
        functools.partial(finish_kernel, first_head),
        out_shape=jax.ShapeDtypeStruct(so_far.shape, so_far.dtype),
        in_specs=[SMEM] + [VMEM] * len(blocks) + [HBM],
        out_specs=HBM,
        scratch_shapes=[pltpu.SemaphoreType.DMA(())],
        input_output_aliases={1 + len(blocks): 0},
        compiler_params=pltpu.CompilerParams(vmem_limit_bytes=4 * MIB),
        cost_estimate=pl.CostEstimate(flops=0, bytes_accessed=so_far.size // 2, transcendentals=0),
        name="finish",
    )(meta, *blocks, so_far)


def shards(queries, keys, values, labels, band):
    frames = lax.axis_size("frame") // 2
    reach = frames // 4

    keys_far = swap_bit(keys, 0)
    values_far = swap_bit(values, 0)
    meta, choice, pair_keep, high_send, low_send, query_keep, query_send = extract(
        reach, labels, band, queries, keys, values
    )

    def attend_piece(result, number):
        first, count = sum(SPATIAL_PIECES[:number]), SPATIAL_PIECES[number]
        return spatial_piece(meta, first, count, queries, keys, values, keys_far, values_far, result)

    def both_swaps(held, distance):
        return swap_pairs(held[1], 0, distance), swap_pairs(held[0], 1, distance)

    own = both_swaps((pair_keep, pair_keep), 1)
    high_got = swap_bit(high_send, 1)
    low_got = swap_bit(low_send, 1)
    result = attend_piece(None, 0)
    high_got, result = lax.optimization_barrier((high_got, result))
    high = both_swaps((high_got, high_got), 1)
    result = attend_piece(result, 1)
    own, low_got, query_send, choice, result = lax.optimization_barrier((own, low_got, query_send, choice, result))
    low = both_swaps((low_got, low_got), 1)
    high_pairs = [pair_keep, high_got, own[0], high[0], own[1], high[1]]
    low_pairs = [pair_keep, low_got, own[0], low[0], own[1], low[1]]
    for distance in range(2, reach):
        own, high, low = (both_swaps(held, distance) for held in (own, high, low))
        high_pairs += [own[0], high[0], own[1], high[1]]
        low_pairs += [own[0], low[0], own[1], low[1]]
    own_last = both_swaps((own[0][:HIGH], own[1][:HIGH]), reach)
    high, result = lax.optimization_barrier((high, result))
    choice = largest(choice)
    query_got = swap_bit(query_send, 1)
    result = attend_piece(result, 2)
    own, high, low, own_last, query_got, choice, result = lax.optimization_barrier(
        (own, high, low, own_last, query_got, choice, result)
    )

    def last_swaps(size, result, meta, own, high, low, own_last, query_keep, query_got, high_pairs, low_pairs):
        attend = functools.partial(temporal, meta, frames, reach)
        high_last = both_swaps(high, reach)
        with_items = min(HIGH + size, TEMP_HEADS)
        early, parts = None, []
        if size:
            for_a, for_b = pack(meta, reach, size, own, low)
            items = [swap_pairs(for_a, 0, reach), swap_pairs(for_b, 1, reach)]
        if with_items < TEMP_HEADS:
            result, send = attend((with_items, TEMP_HEADS), query_keep, query_got, low_pairs, [], result)
            early = with_items, swap_bit(send, 1)
        result, send = attend((0, HIGH), query_keep, query_got, high_pairs, [*own_last, *high_last], result)
        parts.append(swap_bit(send, 1))
        if size:
            result, send = attend((HIGH, with_items), query_keep, query_got, low_pairs, items, result, early)
            parts.append(swap_bit(send, 1))
        else:
            parts.append(early[1])
        return finish(meta, 0, parts, result)

    return lax.switch(
        choice[0], [functools.partial(last_swaps, size) for size in LEVELS],
        result, meta, own, high, low, own_last, query_keep, query_got, high_pairs, low_pairs,
    )


def solution(mesh):
    placed = (
        P(("group", "frame"), None),
        P(("group", "frame"), None),
        P(("group", "frame"), None),
        P("group"),
        P("group"),
    )
    return jax.shard_map(
        shards, mesh=mesh, in_specs=placed, out_specs=P(("group", "frame"), None), check_vma=False
    )
```

```python
import functools
import math

import jax
import jax.numpy as jnp
from jax import lax
from jax.experimental import pallas as pl
from jax.experimental.pallas import tpu as pltpu
from jax.sharding import PartitionSpec as P

TEMP_HEADS = 10
HEAD_DIM = 128
PIXEL_BLOCK = 32
SPATIAL_PIECES = (9, 9, 12)
STEP_HEADS = 3
HIGH = 5
LEVELS = (0, 2, 3, 4, 5, 6, 2 * (TEMP_HEADS - HIGH))
MASKED = -1e30
MIB = 1024 * 1024
HBM = pl.BlockSpec(memory_space=pltpu.HBM)
SMEM = pl.BlockSpec(memory_space=pltpu.SMEM)
VMEM = pl.BlockSpec(memory_space=pltpu.VMEM)


def swap_bit(block, bit):
    count = lax.axis_size("frame")
    return lax.ppermute(block, "frame", [(i, i ^ (1 << bit)) for i in range(count)])


def swap_pairs(block, first, distance):
    count = lax.axis_size("frame")
    places = count // 4
    route = []
    for low in range(first, places - 1, 2):
        if low - (distance - 1) >= 0:
            route += [(low * 4 + i, low * 4 + 4 + i) for i in range(4)]
        if low + distance < places:
            route += [(low * 4 + 4 + i, low * 4 + i) for i in range(4)]
    return lax.ppermute(block, "frame", route)


def largest(value):
    count = lax.axis_size("group")
    result = value
    for shift in range(1, count):
        route = [(i, (i + shift) % count) for i in range(count)]
        result = jnp.maximum(result, lax.ppermute(value, "group", route))
    return result


def position():
    index = lax.axis_index("frame")
    return (index // 2) % 2, index // 4


def columns_of(head):
    return pl.ds(pl.multiple_of(head * HEAD_DIM, HEAD_DIM), HEAD_DIM)


def rows_of(side, half):
    return pl.ds(pl.multiple_of(side * half, half), half)


def extract_kernel(
    reach, labels_hbm, band_hbm, keys, values,
    meta, choice, pair_keep, high_send, low_send, labels, band, found, sems,
):
    heads = labels.shape[0]
    half = pair_keep.shape[2]
    side, _ = position()
    small = [
        pltpu.make_async_copy(labels_hbm, labels, sems.at[0]),
        pltpu.make_async_copy(band_hbm, band, sems.at[1]),
    ]
    for copy in small:
        copy.start()
    for copy in small:
        copy.wait()

    temporal = jnp.int32(0)
    for head in range(heads):
        found[temporal] = head
        temporal = temporal + labels[head]
    listed_heads = [found[number] for number in range(TEMP_HEADS)]
    bands = [band[head] for head in listed_heads]
    kept, sent = rows_of(side, half), rows_of(1 - side, half)
    for number, head in enumerate(listed_heads):
        rank = jnp.int32(0)
        for other in range(TEMP_HEADS):
            if other != number:
                before = bands[other] >= bands[number] if other < number else bands[other] > bands[number]
                rank = rank + before.astype(jnp.int32)
        meta[heads + rank] = head
        meta[2 * heads + rank] = bands[number]
        columns = columns_of(head)
        for kind, source in enumerate((keys, values)):
            pltpu.make_async_copy(source.at[kept, columns], pair_keep.at[rank, kind], sems.at[2]).start()

            @pl.when(rank < HIGH)
            def _():
                pltpu.make_async_copy(source.at[sent, columns], high_send.at[rank, kind], sems.at[3]).start()

            @pl.when(rank >= HIGH)
            def _():
                pltpu.make_async_copy(source.at[sent, columns], low_send.at[rank - HIGH, kind], sems.at[4]).start()

    spatial = jnp.int32(0)
    for head in range(heads):
        meta[spatial] = head
        spatial = jnp.minimum(spatial + 1 - labels[head], heads - TEMP_HEADS)
    items = 3 * heads
    places = items + 2 * TEMP_HEADS
    for number in range(2 * TEMP_HEADS):
        meta[items + number] = 0
    listed = jnp.int32(0)
    for number in range(TEMP_HEADS - HIGH):
        for kind in range(2):
            is_needed = meta[2 * heads + HIGH + number] >= 2 * reach - 1 + kind
            meta[places + 2 * number + kind] = listed

            @pl.when(is_needed)
            def _():
                meta[items + listed] = 2 * number + kind

            listed = listed + is_needed.astype(jnp.int32)
    choice[0] = sum((listed > level).astype(jnp.int32) for level in LEVELS[:-1])
    for number, whole in enumerate((pair_keep, high_send, low_send)):
        pltpu.make_async_copy(whole, whole, sems.at[2 + number]).wait()


def extract(reach, labels, band, keys, values):
    half = keys.shape[0] // 2
    pair = [
        jax.ShapeDtypeStruct((count, 2, half, HEAD_DIM), jnp.bfloat16)
        for count in (TEMP_HEADS, HIGH, TEMP_HEADS - HIGH)
    ]
    return pl.pallas_call(
        functools.partial(extract_kernel, reach),
        out_shape=(
            jax.ShapeDtypeStruct((3 * labels.shape[0] + 4 * TEMP_HEADS,), jnp.int32),
            jax.ShapeDtypeStruct((1,), jnp.int32),
            *pair,
        ),
        in_specs=[HBM] * 4,
        out_specs=(SMEM, SMEM) + (VMEM,) * 3,
        scratch_shapes=[
            pltpu.SMEM(labels.shape, jnp.int32),
            pltpu.SMEM(band.shape, jnp.int32),
            pltpu.SMEM((TEMP_HEADS + 1,), jnp.int32),
            pltpu.SemaphoreType.DMA((5,)),
        ],
        compiler_params=pltpu.CompilerParams(vmem_limit_bytes=58 * MIB),
        cost_estimate=pl.CostEstimate(flops=0, bytes_accessed=8 * TEMP_HEADS * half * HEAD_DIM * 2, transcendentals=0),
        name="extract_temporal",
    )(labels, band, keys, values)


def queries_kernel(meta, queries, query_keep, query_send, sems):
    heads = (meta.shape[0] - 4 * TEMP_HEADS) // 3
    half = query_keep.shape[1]
    side, _ = position()
    kept, sent = rows_of(side, half), rows_of(1 - side, half)
    for number in range(TEMP_HEADS):
        columns = columns_of(meta[heads + number])
        pltpu.make_async_copy(queries.at[kept, columns], query_keep.at[number], sems.at[0]).start()
        pltpu.make_async_copy(queries.at[sent, columns], query_send.at[number], sems.at[1]).start()
    for number, whole in enumerate((query_keep, query_send)):
        pltpu.make_async_copy(whole, whole, sems.at[number]).wait()


def extract_queries(meta, queries):
    half = queries.shape[0] // 2
    single = jax.ShapeDtypeStruct((TEMP_HEADS, half, HEAD_DIM), jnp.bfloat16)
    return pl.pallas_call(
        queries_kernel,
        out_shape=(single, single),
        in_specs=[SMEM, HBM],
        out_specs=(VMEM, VMEM),
        scratch_shapes=[pltpu.SemaphoreType.DMA((2,))],
        compiler_params=pltpu.CompilerParams(vmem_limit_bytes=50 * MIB),
        cost_estimate=pl.CostEstimate(flops=0, bytes_accessed=4 * TEMP_HEADS * half * HEAD_DIM * 2, transcendentals=0),
        name="extract_queries",
    )(meta, queries)


def spatial_kernel(scale, first, meta, *refs):
    heads = [refs[5 * number : 5 * number + 5] for number in range(STEP_HEADS)]
    out, key_all, value_all, held, sems = refs[-5:]
    step, steps = pl.program_id(0), pl.num_programs(0)
    slot = step % 2
    rows = held.shape[2]
    half = rows // 2

    def store(step, slot, number):
        columns = columns_of(meta[first + step * STEP_HEADS + number])
        return pltpu.make_async_copy(held.at[slot, number], out.at[:, columns], sems.at[slot, number])

    @pl.when(step >= 2)
    def _():
        for number in range(STEP_HEADS):
            store(step - 2, slot, number).wait()

    for number, (_, key_own, value_own, key_far, value_far) in enumerate(heads):
        key_all[number, :rows, :] = key_own[...]
        key_all[number, rows:, :] = key_far[...]
        value_all[number, :rows, :HEAD_DIM] = value_own[...]
        value_all[number, rows:, :HEAD_DIM] = value_far[...]
        value_all[number, :, HEAD_DIM:] = jnp.ones((2 * rows, HEAD_DIM), jnp.bfloat16)
    parts = [(number, slice(start, start + half)) for number in range(STEP_HEADS) for start in (0, half)]
    scores = [
        lax.dot_general(
            heads[number][0][part, :], key_all[number], (((1,), (1,)), ((), ())), preferred_element_type=jnp.float32
        )
        for number, part in parts
    ]
    for (number, part), score in zip(parts, scores):
        peak = jnp.max(score, axis=1, keepdims=True)
        weights = jnp.exp2((score - peak) * scale).astype(jnp.bfloat16)
        both = jnp.dot(weights, value_all[number], preferred_element_type=jnp.float32)
        held[slot, number, part, :] = (both[:, :HEAD_DIM] / both[:, HEAD_DIM:]).astype(jnp.bfloat16)
    for number in range(STEP_HEADS):
        store(step, slot, number).start()

    @pl.when(step == steps - 1)
    def _():
        for number in range(STEP_HEADS):
            store(step, slot, number).wait()

    @pl.when((step == steps - 1) & (steps >= 2))
    def _():
        for number in range(STEP_HEADS):
            store(step - 1, 1 - slot, number).wait()


def spatial_piece(meta, first, count, queries, keys, values, keys_far, values_far, so_far):
    rows = queries.shape[0]
    operands, specs = [], []
    for number in range(STEP_HEADS):
        place = lambda i, meta, number=number: (0, meta[first + i * STEP_HEADS + number])
        operands += [queries, keys, values, keys_far, values_far]
        specs += [pl.BlockSpec((rows, HEAD_DIM), place)] * 5
    aliases = {}
    if so_far is not None:
        operands.append(so_far)
        specs.append(HBM)
        aliases = {len(operands): 0}
    return pl.pallas_call(
        functools.partial(spatial_kernel, math.log2(math.e) / math.sqrt(HEAD_DIM), first),
        out_shape=jax.ShapeDtypeStruct(queries.shape, jnp.bfloat16),
        grid_spec=pltpu.PrefetchScalarGridSpec(
            num_scalar_prefetch=1,
            grid=(count // STEP_HEADS,),
            in_specs=specs,
            out_specs=HBM,
            scratch_shapes=[
                pltpu.VMEM((STEP_HEADS, 2 * rows, HEAD_DIM), jnp.bfloat16),
                pltpu.VMEM((STEP_HEADS, 2 * rows, 2 * HEAD_DIM), jnp.bfloat16),
                pltpu.VMEM((2, STEP_HEADS, rows, HEAD_DIM), jnp.bfloat16),
                pltpu.SemaphoreType.DMA((2, STEP_HEADS)),
            ],
        ),
        input_output_aliases=aliases,
        compiler_params=pltpu.CompilerParams(vmem_limit_bytes=50 * MIB),
        cost_estimate=pl.CostEstimate(
            flops=count * rows * 2 * rows * HEAD_DIM * 4,
            bytes_accessed=count * 6 * rows * HEAD_DIM * 2,
            transcendentals=count * rows * 2 * rows,
        ),
        name="spatial_heads",
    )(meta, *operands)


def pack_kernel(reach, meta, own_a, low_a, own_b, low_b, for_a, for_b, sems):
    heads = (meta.shape[0] - 4 * TEMP_HEADS) // 3
    side, place = position()
    even = place % 2 == 0
    sources = (
        (jnp.where(even, place + reach - 1, place - reach + 1), own_a, low_a, for_b, sems.at[0]),
        (jnp.where(even, place - reach + 1, place + reach - 1), own_b, low_b, for_a, sems.at[1]),
    )

    def one_item(number, carry):
        item = meta[3 * heads + number]
        head, kind = item // 2, item % 2
        for origin, own, low, out, sem in sources:
            near = (origin < reach).astype(jnp.int32)
            is_own = (near + kind + side) % 2 == 0

            @pl.when(is_own)
            def _():
                pltpu.make_async_copy(own.at[HIGH + head], out.at[number], sem).start()

            @pl.when(jnp.logical_not(is_own))
            def _():
                pltpu.make_async_copy(low.at[head], out.at[number], sem).start()

        return carry

    lax.fori_loop(0, for_a.shape[0], one_item, jnp.int32(0))
    pltpu.make_async_copy(for_a, for_a, sems.at[1]).wait()
    pltpu.make_async_copy(for_b, for_b, sems.at[0]).wait()


def pack(meta, reach, size, own, low):
    out = jax.ShapeDtypeStruct((size,) + low[0].shape[1:], jnp.bfloat16)
    return pl.pallas_call(
        functools.partial(pack_kernel, reach),
        out_shape=(out, out),
        in_specs=[SMEM] + [HBM] * 4,
        out_specs=(VMEM, VMEM),
        scratch_shapes=[pltpu.SemaphoreType.DMA((2,))],
        compiler_params=pltpu.CompilerParams(vmem_limit_bytes=12 * MIB),
        name="pack_items",
    )(meta, own[0], low[0], own[1], low[1])


def temporal_kernel(scale, frames, reach, first_head, stores, meta, query_own, query_far, *rest):
    if stores:
        refs, (_, out, out_far, out_own, sem) = rest[:-5], rest[-5:]
    else:
        refs, (out_own, out_far) = rest[:-2], rest[-2:]
    count, half = out_far.shape[:2]
    is_high = first_head < HIGH
    heads = (meta.shape[0] - 4 * TEMP_HEADS) // 3
    first_listed = 0 if is_high else HIGH
    side, place = position()
    odd = place % 2 == 1
    size = PIXEL_BLOCK

    shifts = [jnp.int32(0)]
    for distance in range(1, reach):
        up = jnp.where(odd, -distance, distance)
        shifts += [up, -up]
    pairs, last = refs[: 2 * len(shifts)], refs[2 * len(shifts) :]
    lower = place < reach
    from_a = lower != odd
    if last:
        shifts.append(jnp.where(lower, reach, -reach))
    slots = 2 * len(shifts)
    row = lax.broadcasted_iota(jnp.int32, (2 * size, 1), 0)
    column = lax.broadcasted_iota(jnp.int32, (1, slots * size), 1)
    row_frame = jnp.where(row >= size, 1 - side, side) + 2 * place
    slot = column // size
    shift = jnp.zeros_like(slot)
    for number, step in enumerate(shifts):
        shift = jnp.where(slot // 2 == number, step, shift)
    first_of = side
    if last and not is_high:
        first_of = jnp.where(slot // 2 == len(shifts) - 1, jnp.where(lower, 0, 1), side)
    column_frame = jnp.where(slot % 2 == 1, 1 - first_of, first_of) + 2 * (place + shift)
    far = 4 * frames
    column_frame = jnp.where((column_frame >= 0) & (column_frame < frames), column_frame, far)
    apart = jnp.where(row % size == column % size, jnp.abs(row_frame - column_frame), far)
    parts = [slice(start, start + size) for start in range(0, half, size)]

    def one_head(number, carry):
        head = first_head + number
        keep = apart <= meta[2 * heads + head]

        def stacked(kind, part):
            blocks = [pair[head if pair.shape[0] == TEMP_HEADS else head - first_listed, kind, part, :] for pair in pairs]
            if is_high:
                for by_a, by_b in (last[:2], last[2:]):
                    blocks.append(jnp.where(from_a, by_a[head, kind, part, :], by_b[head, kind, part, :]))
            elif last:
                for which in range(2):
                    item = meta[3 * heads + 2 * TEMP_HEADS + 2 * (head - HIGH) + which]
                    item = jnp.minimum(item, last[0].shape[0] - 1)
                    by_a, by_b = (block[item, kind, part, :] for block in last)
                    blocks.append(jnp.where(from_a, by_a, by_b))
            return jnp.concatenate(blocks, axis=0)

        scores = []
        for part in parts:
            query = jnp.concatenate([query_own[head, part, :], query_far[head, part, :]], axis=0)
            score = lax.dot_general(
                query, stacked(0, part), (((1,), (1,)), ((), ())), preferred_element_type=jnp.float32
            )
            scores.append(jnp.where(keep, score, MASKED))
        weights = []
        for score in scores:
            peak = jnp.max(score, axis=1, keepdims=True)
            weight = jnp.exp2((score - peak) * scale)
            weights.append((weight.astype(jnp.bfloat16), jnp.sum(weight, axis=1, keepdims=True)))
        results = [
            jnp.dot(weight, stacked(1, part), preferred_element_type=jnp.float32) / total
            for part, (weight, total) in zip(parts, weights)
        ]
        for part, result in zip(parts, results):
            out_own[number, part, :] = result[:size].astype(jnp.bfloat16)
            out_far[number, part, :] = result[size:].astype(jnp.bfloat16)
        if stores:
            columns = columns_of(meta[heads + head])
            pltpu.make_async_copy(out_own.at[number], out.at[rows_of(side, half), columns], sem).start()
        return carry

    lax.fori_loop(0, count, one_head, jnp.int32(0))
    if stores:
        pltpu.make_async_copy(out_own, out_own, sem).wait()


def temporal(meta, frames, reach, heads, query_own, query_far, pairs, last, so_far=None):
    first_head, end = heads
    count, half = end - first_head, query_own.shape[1]
    stores = so_far is not None
    operands = [meta, query_own, query_far, *pairs, *last]
    specs = [SMEM] + [VMEM] * (len(operands) - 1)
    block = jax.ShapeDtypeStruct((count, half, HEAD_DIM), jnp.bfloat16)
    outs, out_specs, scratch = (block, block), (VMEM, VMEM), []
    if stores:
        operands.append(so_far)
        specs.append(HBM)
        outs, out_specs = (jax.ShapeDtypeStruct(so_far.shape, so_far.dtype), block), (HBM, VMEM)
        scratch = [pltpu.VMEM(block.shape, block.dtype), pltpu.SemaphoreType.DMA(())]
    slots = 2 + len(pairs)
    return pl.pallas_call(
        functools.partial(
            temporal_kernel, math.log2(math.e) / math.sqrt(HEAD_DIM), frames, reach, first_head, stores
        ),
        out_shape=outs,
        in_specs=specs,
        out_specs=out_specs,
        scratch_shapes=scratch,
        input_output_aliases={len(operands) - 1: 0} if stores else {},
        compiler_params=pltpu.CompilerParams(vmem_limit_bytes=44 * MIB),
        cost_estimate=pl.CostEstimate(
            flops=count * half * slots * PIXEL_BLOCK * HEAD_DIM * 8,
            bytes_accessed=count * half * HEAD_DIM * 2 * (4 + 2 * slots),
            transcendentals=count * half * 2 * slots * PIXEL_BLOCK,
        ),
        name="temporal_heads",
    )(*operands)


def finish_kernel(plan, meta, *refs):
    blocks, (_, out, sem) = refs[:-3], refs[-3:]
    heads = (meta.shape[0] - 4 * TEMP_HEADS) // 3
    side, _ = position()
    for block, (head, came_back) in zip(blocks, plan):
        count, half = block.shape[:2]
        rows = rows_of(1 - side if came_back else side, half)
        for number in range(count):
            columns = columns_of(meta[heads + head + number])
            pltpu.make_async_copy(block.at[number], out.at[rows, columns], sem).start()
    for block in blocks:
        pltpu.make_async_copy(block, block, sem).wait()


def finish(meta, parts, so_far):
    blocks = [block for block, _, _ in parts]
    return pl.pallas_call(
        functools.partial(finish_kernel, [(head, came_back) for _, head, came_back in parts]),
        out_shape=jax.ShapeDtypeStruct(so_far.shape, so_far.dtype),
        in_specs=[SMEM] + [VMEM] * len(blocks) + [HBM],
        out_specs=HBM,
        scratch_shapes=[pltpu.SemaphoreType.DMA(())],
        input_output_aliases={1 + len(blocks): 0},
        compiler_params=pltpu.CompilerParams(vmem_limit_bytes=4 * MIB),
        cost_estimate=pl.CostEstimate(flops=0, bytes_accessed=so_far.size // 2, transcendentals=0),
        name="finish",
    )(meta, *blocks, so_far)


def shards(queries, keys, values, labels, band):
    frames = lax.axis_size("frame") // 2
    reach = frames // 4

    keys_far = swap_bit(keys, 0)
    values_far = swap_bit(values, 0)
    meta, choice, pair_keep, high_send, low_send = extract(reach, labels, band, keys, values)

    def attend_piece(result, number):
        first, count = sum(SPATIAL_PIECES[:number]), SPATIAL_PIECES[number]
        return spatial_piece(meta, first, count, queries, keys, values, keys_far, values_far, result)

    def both_swaps(held, distance):
        return swap_pairs(held[1], 0, distance), swap_pairs(held[0], 1, distance)

    own = both_swaps((pair_keep, pair_keep), 1)
    high_got = swap_bit(high_send, 1)
    low_got = swap_bit(low_send, 1)
    result = attend_piece(None, 0)
    meta_then, result = lax.optimization_barrier((meta, result))
    query_keep, query_send = extract_queries(meta_then, queries)
    high_got, query_send, result = lax.optimization_barrier((high_got, query_send, result))
    high = both_swaps((high_got, high_got), 1)
    result = attend_piece(result, 1)
    own, low_got, query_send, choice, result = lax.optimization_barrier((own, low_got, query_send, choice, result))
    low = both_swaps((low_got, low_got), 1)
    high_pairs = [pair_keep, high_got, own[0], high[0], own[1], high[1]]
    low_pairs = [pair_keep, low_got, own[0], low[0], own[1], low[1]]
    for distance in range(2, reach):
        own, high, low = (both_swaps(held, distance) for held in (own, high, low))
        high_pairs += [own[0], high[0], own[1], high[1]]
        low_pairs += [own[0], low[0], own[1], low[1]]
    own_last = both_swaps((own[0][:HIGH], own[1][:HIGH]), reach)
    high, result = lax.optimization_barrier((high, result))
    choice = largest(choice)
    query_got = swap_bit(query_send, 1)
    result = attend_piece(result, 2)
    own, high, low, own_last, query_got, choice, result = lax.optimization_barrier(
        (own, high, low, own_last, query_got, choice, result)
    )

    def last_swaps(size, result, meta, own, high, low, own_last, query_keep, query_got, high_pairs, low_pairs):
        attend = functools.partial(temporal, meta, frames, reach)
        high_last = both_swaps(high, reach)
        with_items = min(HIGH + size, TEMP_HEADS)
        parts = []
        if with_items < TEMP_HEADS:
            result, send = attend((with_items, TEMP_HEADS), query_keep, query_got, low_pairs, [], result)
            parts.append((swap_bit(send, 1), with_items, True))
            meta_then, query_keep, _ = lax.optimization_barrier((meta, query_keep, send))
        else:
            meta_then = meta
        if size:
            for_a, for_b = pack(meta_then, reach, size, own, low)
            items = [swap_pairs(for_a, 0, reach), swap_pairs(for_b, 1, reach)]
        keep, send = attend((0, HIGH), query_keep, query_got, high_pairs, [*own_last, *high_last])
        parts += [(keep, 0, False), (swap_bit(send, 1), 0, True)]
        if size:
            query_keep, *_ = lax.optimization_barrier((query_keep, send, [block for block, _, _ in parts[:-1]]))
            keep, send = attend((HIGH, with_items), query_keep, query_got, low_pairs, items)
            parts += [(keep, HIGH, False), (swap_bit(send, 1), HIGH, True)]
        return finish(meta, parts, result)

    return lax.switch(
        choice[0], [functools.partial(last_swaps, size) for size in LEVELS],
        result, meta, own, high, low, own_last, query_keep, query_got, high_pairs, low_pairs,
    )


def solution(mesh):
    placed = (
        P(("group", "frame"), None),
        P(("group", "frame"), None),
        P(("group", "frame"), None),
        P("group"),
        P("group"),
    )
    return jax.shard_map(
        shards, mesh=mesh, in_specs=placed, out_specs=P(("group", "frame"), None), check_vma=False
    )
```

```python
import functools
import math

import jax
import jax.numpy as jnp
from jax import lax
from jax.experimental import pallas as pl
from jax.experimental.pallas import tpu as pltpu
from jax.sharding import PartitionSpec as P

TEMP_HEADS = 10
HEAD_DIM = 128
PIXEL_BLOCK = 32
SPATIAL_PIECES = (9, 6, 15)
STEP_HEADS = 3
HIGH = 5
LEVELS = (0, 2, 3, 4, 5, 6, 2 * (TEMP_HEADS - HIGH))
MASKED = -1e30
MIB = 1024 * 1024
HBM = pl.BlockSpec(memory_space=pltpu.HBM)
SMEM = pl.BlockSpec(memory_space=pltpu.SMEM)
VMEM = pl.BlockSpec(memory_space=pltpu.VMEM)


def swap_bit(block, bit):
    count = lax.axis_size("frame")
    return lax.ppermute(block, "frame", [(i, i ^ (1 << bit)) for i in range(count)])


def swap_pairs(block, first, distance):
    count = lax.axis_size("frame")
    places = count // 4
    route = []
    for low in range(first, places - 1, 2):
        if low - (distance - 1) >= 0:
            route += [(low * 4 + i, low * 4 + 4 + i) for i in range(4)]
        if low + distance < places:
            route += [(low * 4 + 4 + i, low * 4 + i) for i in range(4)]
    return lax.ppermute(block, "frame", route)


def largest(value):
    count = lax.axis_size("group")
    result = value
    for shift in range(1, count):
        route = [(i, (i + shift) % count) for i in range(count)]
        result = jnp.maximum(result, lax.ppermute(value, "group", route))
    return result


def position():
    index = lax.axis_index("frame")
    return (index // 2) % 2, index // 4


def columns_of(head):
    return pl.ds(pl.multiple_of(head * HEAD_DIM, HEAD_DIM), HEAD_DIM)


def rows_of(side, half):
    return pl.ds(pl.multiple_of(side * half, half), half)


def extract_kernel(
    reach, labels_hbm, band_hbm, keys, values,
    meta, choice, pair_keep, high_send, low_send, labels, band, found, sems,
):
    heads = labels.shape[0]
    half = pair_keep.shape[2]
    side, _ = position()
    small = [
        pltpu.make_async_copy(labels_hbm, labels, sems.at[0]),
        pltpu.make_async_copy(band_hbm, band, sems.at[1]),
    ]
    for copy in small:
        copy.start()
    for copy in small:
        copy.wait()

    temporal = jnp.int32(0)
    for head in range(heads):
        found[temporal] = head
        temporal = temporal + labels[head]
    listed_heads = [found[number] for number in range(TEMP_HEADS)]
    bands = [band[head] for head in listed_heads]
    kept, sent = rows_of(side, half), rows_of(1 - side, half)
    for number, head in enumerate(listed_heads):
        rank = jnp.int32(0)
        for other in range(TEMP_HEADS):
            if other != number:
                before = bands[other] >= bands[number] if other < number else bands[other] > bands[number]
                rank = rank + before.astype(jnp.int32)
        meta[heads + rank] = head
        meta[2 * heads + rank] = bands[number]
        columns = columns_of(head)
        for kind, source in enumerate((keys, values)):
            pltpu.make_async_copy(source.at[kept, columns], pair_keep.at[rank, kind], sems.at[2]).start()

            @pl.when(rank < HIGH)
            def _():
                pltpu.make_async_copy(source.at[sent, columns], high_send.at[rank, kind], sems.at[3]).start()

            @pl.when(rank >= HIGH)
            def _():
                pltpu.make_async_copy(source.at[sent, columns], low_send.at[rank - HIGH, kind], sems.at[4]).start()

    spatial = jnp.int32(0)
    for head in range(heads):
        meta[spatial] = head
        spatial = jnp.minimum(spatial + 1 - labels[head], heads - TEMP_HEADS)
    items = 3 * heads
    places = items + 2 * TEMP_HEADS
    for number in range(2 * TEMP_HEADS):
        meta[items + number] = 0
    listed = jnp.int32(0)
    for number in range(TEMP_HEADS - HIGH):
        for kind in range(2):
            is_needed = meta[2 * heads + HIGH + number] >= 2 * reach - 1 + kind
            meta[places + 2 * number + kind] = listed

            @pl.when(is_needed)
            def _():
                meta[items + listed] = 2 * number + kind

            listed = listed + is_needed.astype(jnp.int32)
    choice[0] = sum((listed > level).astype(jnp.int32) for level in LEVELS[:-1])
    for number, whole in enumerate((pair_keep, high_send, low_send)):
        pltpu.make_async_copy(whole, whole, sems.at[2 + number]).wait()


def extract(reach, labels, band, keys, values):
    half = keys.shape[0] // 2
    pair = [
        jax.ShapeDtypeStruct((count, 2, half, HEAD_DIM), jnp.bfloat16)
        for count in (TEMP_HEADS, HIGH, TEMP_HEADS - HIGH)
    ]
    return pl.pallas_call(
        functools.partial(extract_kernel, reach),
        out_shape=(
            jax.ShapeDtypeStruct((3 * labels.shape[0] + 4 * TEMP_HEADS,), jnp.int32),
            jax.ShapeDtypeStruct((1,), jnp.int32),
            *pair,
        ),
        in_specs=[HBM] * 4,
        out_specs=(SMEM, SMEM) + (VMEM,) * 3,
        scratch_shapes=[
            pltpu.SMEM(labels.shape, jnp.int32),
            pltpu.SMEM(band.shape, jnp.int32),
            pltpu.SMEM((TEMP_HEADS + 1,), jnp.int32),
            pltpu.SemaphoreType.DMA((5,)),
        ],
        compiler_params=pltpu.CompilerParams(vmem_limit_bytes=58 * MIB),
        cost_estimate=pl.CostEstimate(flops=0, bytes_accessed=8 * TEMP_HEADS * half * HEAD_DIM * 2, transcendentals=0),
        name="extract_temporal",
    )(labels, band, keys, values)


def queries_kernel(meta, queries, query_keep, query_send, sems):
    heads = (meta.shape[0] - 4 * TEMP_HEADS) // 3
    half = query_keep.shape[1]
    side, _ = position()
    kept, sent = rows_of(side, half), rows_of(1 - side, half)
    for number in range(TEMP_HEADS):
        columns = columns_of(meta[heads + number])
        pltpu.make_async_copy(queries.at[kept, columns], query_keep.at[number], sems.at[0]).start()
        pltpu.make_async_copy(queries.at[sent, columns], query_send.at[number], sems.at[1]).start()
    for number, whole in enumerate((query_keep, query_send)):
        pltpu.make_async_copy(whole, whole, sems.at[number]).wait()


def extract_queries(meta, queries):
    half = queries.shape[0] // 2
    single = jax.ShapeDtypeStruct((TEMP_HEADS, half, HEAD_DIM), jnp.bfloat16)
    return pl.pallas_call(
        queries_kernel,
        out_shape=(single, single),
        in_specs=[SMEM, HBM],
        out_specs=(VMEM, VMEM),
        scratch_shapes=[pltpu.SemaphoreType.DMA((2,))],
        compiler_params=pltpu.CompilerParams(vmem_limit_bytes=50 * MIB),
        cost_estimate=pl.CostEstimate(flops=0, bytes_accessed=4 * TEMP_HEADS * half * HEAD_DIM * 2, transcendentals=0),
        name="extract_queries",
    )(meta, queries)


def spatial_kernel(scale, first, meta, *refs):
    heads = [refs[5 * number : 5 * number + 5] for number in range(STEP_HEADS)]
    out, held, sems = refs[-3:]
    step, steps = pl.program_id(0), pl.num_programs(0)
    slot = step % 2
    rows = held.shape[2]
    half = rows // 2

    def store(step, slot, number):
        columns = columns_of(meta[first + step * STEP_HEADS + number])
        return pltpu.make_async_copy(held.at[slot, number], out.at[:, columns], sems.at[slot, number])

    @pl.when(step >= 2)
    def _():
        for number in range(STEP_HEADS):
            store(step - 2, slot, number).wait()

    key = [jnp.concatenate([key_own[...], key_far[...]], axis=0) for _, key_own, _, key_far, _ in heads]
    value = [jnp.concatenate([value_own[...], value_far[...]], axis=0) for _, _, value_own, _, value_far in heads]
    parts = [(number, slice(start, start + half)) for number in range(STEP_HEADS) for start in (0, half)]
    scores = [
        lax.dot_general(
            heads[number][0][part, :], key[number], (((1,), (1,)), ((), ())), preferred_element_type=jnp.float32
        )
        for number, part in parts
    ]
    for (number, part), score in zip(parts, scores):
        peak = jnp.max(score, axis=1, keepdims=True)
        weights = jnp.exp2((score - peak) * scale)
        total = jnp.sum(weights, axis=1, keepdims=True)
        result = jnp.dot(weights.astype(jnp.bfloat16), value[number], preferred_element_type=jnp.float32)
        held[slot, number, part, :] = (result / total).astype(jnp.bfloat16)
    for number in range(STEP_HEADS):
        store(step, slot, number).start()

    @pl.when(step == steps - 1)
    def _():
        for number in range(STEP_HEADS):
            store(step, slot, number).wait()

    @pl.when((step == steps - 1) & (steps >= 2))
    def _():
        for number in range(STEP_HEADS):
            store(step - 1, 1 - slot, number).wait()


def spatial_piece(meta, first, count, queries, keys, values, keys_far, values_far, so_far):
    rows = queries.shape[0]
    operands, specs = [], []
    for number in range(STEP_HEADS):
        place = lambda i, meta, number=number: (0, meta[first + i * STEP_HEADS + number])
        operands += [queries, keys, values, keys_far, values_far]
        specs += [pl.BlockSpec((rows, HEAD_DIM), place)] * 5
    aliases = {}
    if so_far is not None:
        operands.append(so_far)
        specs.append(HBM)
        aliases = {len(operands): 0}
    return pl.pallas_call(
        functools.partial(spatial_kernel, math.log2(math.e) / math.sqrt(HEAD_DIM), first),
        out_shape=jax.ShapeDtypeStruct(queries.shape, jnp.bfloat16),
        grid_spec=pltpu.PrefetchScalarGridSpec(
            num_scalar_prefetch=1,
            grid=(count // STEP_HEADS,),
            in_specs=specs,
            out_specs=HBM,
            scratch_shapes=[
                pltpu.VMEM((2, STEP_HEADS, rows, HEAD_DIM), jnp.bfloat16),
                pltpu.SemaphoreType.DMA((2, STEP_HEADS)),
            ],
        ),
        input_output_aliases=aliases,
        compiler_params=pltpu.CompilerParams(vmem_limit_bytes=50 * MIB),
        cost_estimate=pl.CostEstimate(
            flops=count * rows * 2 * rows * HEAD_DIM * 4,
            bytes_accessed=count * 6 * rows * HEAD_DIM * 2,
            transcendentals=count * rows * 2 * rows,
        ),
        name="spatial_heads",
    )(meta, *operands)


def pack_kernel(reach, meta, own_a, low_a, own_b, low_b, for_a, for_b, sems):
    heads = (meta.shape[0] - 4 * TEMP_HEADS) // 3
    side, place = position()
    even = place % 2 == 0
    sources = (
        (jnp.where(even, place + reach - 1, place - reach + 1), own_a, low_a, for_b, sems.at[0]),
        (jnp.where(even, place - reach + 1, place + reach - 1), own_b, low_b, for_a, sems.at[1]),
    )

    def one_item(number, carry):
        item = meta[3 * heads + number]
        head, kind = item // 2, item % 2
        for origin, own, low, out, sem in sources:
            near = (origin < reach).astype(jnp.int32)
            is_own = (near + kind + side) % 2 == 0

            @pl.when(is_own)
            def _():
                pltpu.make_async_copy(own.at[HIGH + head], out.at[number], sem).start()

            @pl.when(jnp.logical_not(is_own))
            def _():
                pltpu.make_async_copy(low.at[head], out.at[number], sem).start()

        return carry

    lax.fori_loop(0, for_a.shape[0], one_item, jnp.int32(0))
    pltpu.make_async_copy(for_a, for_a, sems.at[1]).wait()
    pltpu.make_async_copy(for_b, for_b, sems.at[0]).wait()


def pack(meta, reach, size, own, low):
    out = jax.ShapeDtypeStruct((size,) + low[0].shape[1:], jnp.bfloat16)
    return pl.pallas_call(
        functools.partial(pack_kernel, reach),
        out_shape=(out, out),
        in_specs=[SMEM] + [HBM] * 4,
        out_specs=(VMEM, VMEM),
        scratch_shapes=[pltpu.SemaphoreType.DMA((2,))],
        compiler_params=pltpu.CompilerParams(vmem_limit_bytes=12 * MIB),
        name="pack_items",
    )(meta, own[0], low[0], own[1], low[1])


def temporal_kernel(scale, frames, reach, first_head, stores, meta, query_own, query_far, *rest):
    if stores:
        refs, (_, out, out_far, out_own, sem) = rest[:-5], rest[-5:]
    else:
        refs, (out_own, out_far) = rest[:-2], rest[-2:]
    count, half = out_far.shape[:2]
    is_high = first_head < HIGH
    heads = (meta.shape[0] - 4 * TEMP_HEADS) // 3
    first_listed = 0 if is_high else HIGH
    side, place = position()
    odd = place % 2 == 1
    size = PIXEL_BLOCK

    shifts = [jnp.int32(0)]
    for distance in range(1, reach):
        up = jnp.where(odd, -distance, distance)
        shifts += [up, -up]
    pairs, last = refs[: 2 * len(shifts)], refs[2 * len(shifts) :]
    lower = place < reach
    from_a = lower != odd
    if last:
        shifts.append(jnp.where(lower, reach, -reach))
    slots = 2 * len(shifts)
    row = lax.broadcasted_iota(jnp.int32, (2 * size, 1), 0)
    column = lax.broadcasted_iota(jnp.int32, (1, slots * size), 1)
    row_frame = jnp.where(row >= size, 1 - side, side) + 2 * place
    slot = column // size
    shift = jnp.zeros_like(slot)
    for number, step in enumerate(shifts):
        shift = jnp.where(slot // 2 == number, step, shift)
    first_of = side
    if last and not is_high:
        first_of = jnp.where(slot // 2 == len(shifts) - 1, jnp.where(lower, 0, 1), side)
    column_frame = jnp.where(slot % 2 == 1, 1 - first_of, first_of) + 2 * (place + shift)
    far = 4 * frames
    column_frame = jnp.where((column_frame >= 0) & (column_frame < frames), column_frame, far)
    apart = jnp.where(row % size == column % size, jnp.abs(row_frame - column_frame), far)
    parts = [slice(start, start + size) for start in range(0, half, size)]

    def one_head(number, carry):
        head = first_head + number
        keep = apart <= meta[2 * heads + head]

        def stacked(kind, part):
            blocks = [pair[head if pair.shape[0] == TEMP_HEADS else head - first_listed, kind, part, :] for pair in pairs]
            if is_high:
                for by_b, by_a in (last[:2], last[2:]):
                    blocks.append(jnp.where(from_a, by_a[head, kind, part, :], by_b[head, kind, part, :]))
            elif last:
                for which in range(2):
                    item = meta[3 * heads + 2 * TEMP_HEADS + 2 * (head - HIGH) + which]
                    item = jnp.minimum(item, last[0].shape[0] - 1)
                    by_a, by_b = (block[item, kind, part, :] for block in last)
                    blocks.append(jnp.where(from_a, by_a, by_b))
            return jnp.concatenate(blocks, axis=0)

        scores = []
        for part in parts:
            query = jnp.concatenate([query_own[head, part, :], query_far[head, part, :]], axis=0)
            score = lax.dot_general(
                query, stacked(0, part), (((1,), (1,)), ((), ())), preferred_element_type=jnp.float32
            )
            scores.append(jnp.where(keep, score, MASKED))
        weights = []
        for score in scores:
            peak = jnp.max(score, axis=1, keepdims=True)
            weight = jnp.exp2((score - peak) * scale)
            weights.append((weight.astype(jnp.bfloat16), jnp.sum(weight, axis=1, keepdims=True)))
        results = [
            jnp.dot(weight, stacked(1, part), preferred_element_type=jnp.float32) / total
            for part, (weight, total) in zip(parts, weights)
        ]
        for part, result in zip(parts, results):
            out_own[number, part, :] = result[:size].astype(jnp.bfloat16)
            out_far[number, part, :] = result[size:].astype(jnp.bfloat16)
        if stores:
            columns = columns_of(meta[heads + head])
            pltpu.make_async_copy(out_own.at[number], out.at[rows_of(side, half), columns], sem).start()
        return carry

    lax.fori_loop(0, count, one_head, jnp.int32(0))
    if stores:
        pltpu.make_async_copy(out_own, out_own, sem).wait()


def temporal(meta, frames, reach, heads, query_own, query_far, pairs, last, so_far=None):
    first_head, end = heads
    count, half = end - first_head, query_own.shape[1]
    stores = so_far is not None
    operands = [meta, query_own, query_far, *pairs, *last]
    specs = [SMEM] + [VMEM] * (len(operands) - 1)
    block = jax.ShapeDtypeStruct((count, half, HEAD_DIM), jnp.bfloat16)
    outs, out_specs, scratch = (block, block), (VMEM, VMEM), []
    if stores:
        operands.append(so_far)
        specs.append(HBM)
        outs, out_specs = (jax.ShapeDtypeStruct(so_far.shape, so_far.dtype), block), (HBM, VMEM)
        scratch = [pltpu.VMEM(block.shape, block.dtype), pltpu.SemaphoreType.DMA(())]
    slots = 2 + len(pairs)
    return pl.pallas_call(
        functools.partial(
            temporal_kernel, math.log2(math.e) / math.sqrt(HEAD_DIM), frames, reach, first_head, stores
        ),
        out_shape=outs,
        in_specs=specs,
        out_specs=out_specs,
        scratch_shapes=scratch,
        input_output_aliases={len(operands) - 1: 0} if stores else {},
        compiler_params=pltpu.CompilerParams(vmem_limit_bytes=44 * MIB),
        cost_estimate=pl.CostEstimate(
            flops=count * half * slots * PIXEL_BLOCK * HEAD_DIM * 8,
            bytes_accessed=count * half * HEAD_DIM * 2 * (4 + 2 * slots),
            transcendentals=count * half * 2 * slots * PIXEL_BLOCK,
        ),
        name="temporal_heads",
    )(*operands)


def finish_kernel(plan, meta, *refs):
    blocks, (_, out, sem) = refs[:-3], refs[-3:]
    heads = (meta.shape[0] - 4 * TEMP_HEADS) // 3
    side, _ = position()
    for block, (head, came_back) in zip(blocks, plan):
        count, half = block.shape[:2]
        rows = rows_of(1 - side if came_back else side, half)
        for number in range(count):
            columns = columns_of(meta[heads + head + number])
            pltpu.make_async_copy(block.at[number], out.at[rows, columns], sem).start()
    for block in blocks:
        pltpu.make_async_copy(block, block, sem).wait()


def finish(meta, parts, so_far):
    blocks = [block for block, _, _ in parts]
    return pl.pallas_call(
        functools.partial(finish_kernel, [(head, came_back) for _, head, came_back in parts]),
        out_shape=jax.ShapeDtypeStruct(so_far.shape, so_far.dtype),
        in_specs=[SMEM] + [VMEM] * len(blocks) + [HBM],
        out_specs=HBM,
        scratch_shapes=[pltpu.SemaphoreType.DMA(())],
        input_output_aliases={1 + len(blocks): 0},
        compiler_params=pltpu.CompilerParams(vmem_limit_bytes=4 * MIB),
        cost_estimate=pl.CostEstimate(flops=0, bytes_accessed=so_far.size // 2, transcendentals=0),
        name="finish",
    )(meta, *blocks, so_far)


def shards(queries, keys, values, labels, band):
    frames = lax.axis_size("frame") // 2
    reach = frames // 4

    keys_far = swap_bit(keys, 0)
    values_far = swap_bit(values, 0)
    meta, choice, pair_keep, high_send, low_send = extract(reach, labels, band, keys, values)

    def attend_piece(result, number):
        first, count = sum(SPATIAL_PIECES[:number]), SPATIAL_PIECES[number]
        return spatial_piece(meta, first, count, queries, keys, values, keys_far, values_far, result)

    def both_swaps(held, distance):
        return swap_pairs(held[1], 0, distance), swap_pairs(held[0], 1, distance)

    own = both_swaps((pair_keep, pair_keep), 1)
    high_got = swap_bit(high_send, 1)
    low_got = swap_bit(low_send, 1)
    result = attend_piece(None, 0)
    meta_then, result = lax.optimization_barrier((meta, result))
    query_keep, query_send = extract_queries(meta_then, queries)
    high_got, query_send, result = lax.optimization_barrier((high_got, query_send, result))
    high = both_swaps((high_got, high_got), 1)
    result = attend_piece(result, 1)
    own, low_got, query_send, choice, result = lax.optimization_barrier((own, low_got, query_send, choice, result))
    low = both_swaps((low_got, low_got), 1)
    high_pairs = [pair_keep, high_got, own[0], high[0], own[1], high[1]]
    low_pairs = [pair_keep, low_got, own[0], low[0], own[1], low[1]]
    for distance in range(2, reach):
        own, high, low = (both_swaps(held, distance) for held in (own, high, low))
        high_pairs += [own[0], high[0], own[1], high[1]]
        low_pairs += [own[0], low[0], own[1], low[1]]
    own_last = both_swaps((own[0][:HIGH], own[1][:HIGH]), reach)
    own_last = own_last[::-1]
    high, result = lax.optimization_barrier((high, result))
    choice = largest(choice)
    query_got = swap_bit(query_send, 1)
    result = attend_piece(result, 2)
    own, high, low, own_last, query_got, choice, result = lax.optimization_barrier(
        (own, high, low, own_last, query_got, choice, result)
    )

    def last_swaps(size, result, meta, own, high, low, own_last, query_keep, query_got, high_pairs, low_pairs):
        attend = functools.partial(temporal, meta, frames, reach)
        high_last = both_swaps(high, reach)
        with_items = min(HIGH + size, TEMP_HEADS)
        parts = []
        if with_items < TEMP_HEADS:
            result, send = attend((with_items, TEMP_HEADS), query_keep, query_got, low_pairs, [], result)
            parts.append((swap_bit(send, 1), with_items, True))
            meta_then, query_keep, _ = lax.optimization_barrier((meta, query_keep, send))
        else:
            meta_then = meta
        if size:
            for_a, for_b = pack(meta_then, reach, size, own, low)
            items = [swap_pairs(for_a, 0, reach), swap_pairs(for_b, 1, reach)]
        keep, send = attend((0, HIGH), query_keep, query_got, high_pairs, [*own_last, *high_last[::-1]])
        parts += [(keep, 0, False), (swap_bit(send, 1), 0, True)]
        if size:
            query_keep, *_ = lax.optimization_barrier((query_keep, send, [block for block, _, _ in parts[:-1]]))
            keep, send = attend((HIGH, with_items), query_keep, query_got, low_pairs, items)
            parts += [(keep, HIGH, False), (swap_bit(send, 1), HIGH, True)]
        return finish(meta, parts, result)

    return lax.switch(
        choice[0], [functools.partial(last_swaps, size) for size in LEVELS],
        result, meta, own, high, low, own_last, query_keep, query_got, high_pairs, low_pairs,
    )


def solution(mesh):
    placed = (
        P(("group", "frame"), None),
        P(("group", "frame"), None),
        P(("group", "frame"), None),
        P("group"),
        P("group"),
    )
    return jax.shard_map(
        shards, mesh=mesh, in_specs=placed, out_specs=P(("group", "frame"), None), check_vma=False
    )
```

```python
import functools
import math

import jax
import jax.numpy as jnp
from jax import lax
from jax.experimental import pallas as pl
from jax.experimental.pallas import tpu as pltpu
from jax.sharding import PartitionSpec as P

TEMP_HEADS = 10
HEAD_DIM = 128
PIXEL_BLOCK = 32
SPATIAL_PIECES = (9, 6, 15)
STEP_HEADS = 3
HIGH = 5
LEVELS = (0, 2, 3, 4, 5, 6, 2 * (TEMP_HEADS - HIGH))
MASKED = -1e30
MIB = 1024 * 1024
HBM = pl.BlockSpec(memory_space=pltpu.HBM)
SMEM = pl.BlockSpec(memory_space=pltpu.SMEM)
VMEM = pl.BlockSpec(memory_space=pltpu.VMEM)


def swap_bit(block, bit):
    count = lax.axis_size("frame")
    return lax.ppermute(block, "frame", [(i, i ^ (1 << bit)) for i in range(count)])


def swap_pairs(block, first, distance):
    count = lax.axis_size("frame")
    places = count // 4
    route = []
    for low in range(first, places - 1, 2):
        if low - (distance - 1) >= 0:
            route += [(low * 4 + i, low * 4 + 4 + i) for i in range(4)]
        if low + distance < places:
            route += [(low * 4 + 4 + i, low * 4 + i) for i in range(4)]
    return lax.ppermute(block, "frame", route)


def largest(value):
    count = lax.axis_size("group")
    result = value
    for shift in range(1, count):
        route = [(i, (i + shift) % count) for i in range(count)]
        result = jnp.maximum(result, lax.ppermute(value, "group", route))
    return result


def position():
    index = lax.axis_index("frame")
    return (index // 2) % 2, index // 4


def columns_of(head):
    return pl.ds(pl.multiple_of(head * HEAD_DIM, HEAD_DIM), HEAD_DIM)


def rows_of(side, half):
    return pl.ds(pl.multiple_of(side * half, half), half)


def extract_kernel(
    reach, labels_hbm, band_hbm, keys, values,
    meta, choice, pair_keep, labels, band, found, sems,
):
    heads = labels.shape[0]
    half = pair_keep.shape[2]
    side, _ = position()
    small = [
        pltpu.make_async_copy(labels_hbm, labels, sems.at[0]),
        pltpu.make_async_copy(band_hbm, band, sems.at[1]),
    ]
    for copy in small:
        copy.start()
    for copy in small:
        copy.wait()

    temporal = jnp.int32(0)
    for head in range(heads):
        found[temporal] = head
        temporal = temporal + labels[head]
    listed_heads = [found[number] for number in range(TEMP_HEADS)]
    bands = [band[head] for head in listed_heads]
    kept = rows_of(side, half)
    for number, head in enumerate(listed_heads):
        rank = jnp.int32(0)
        for other in range(TEMP_HEADS):
            if other != number:
                before = bands[other] >= bands[number] if other < number else bands[other] > bands[number]
                rank = rank + before.astype(jnp.int32)
        meta[heads + rank] = head
        meta[2 * heads + rank] = bands[number]
        columns = columns_of(head)
        for kind, source in enumerate((keys, values)):
            pltpu.make_async_copy(source.at[kept, columns], pair_keep.at[rank, kind], sems.at[2]).start()

    spatial = jnp.int32(0)
    for head in range(heads):
        meta[spatial] = head
        spatial = jnp.minimum(spatial + 1 - labels[head], heads - TEMP_HEADS)
    items = 3 * heads
    places = items + 2 * TEMP_HEADS
    for number in range(2 * TEMP_HEADS):
        meta[items + number] = 0
    listed = jnp.int32(0)
    for number in range(TEMP_HEADS - HIGH):
        for kind in range(2):
            is_needed = meta[2 * heads + HIGH + number] >= 2 * reach - 1 + kind
            meta[places + 2 * number + kind] = listed

            @pl.when(is_needed)
            def _():
                meta[items + listed] = 2 * number + kind

            listed = listed + is_needed.astype(jnp.int32)
    choice[0] = sum((listed > level).astype(jnp.int32) for level in LEVELS[:-1])
    pltpu.make_async_copy(pair_keep, pair_keep, sems.at[2]).wait()


def extract(reach, labels, band, keys, values):
    half = keys.shape[0] // 2
    pair = jax.ShapeDtypeStruct((TEMP_HEADS, 2, half, HEAD_DIM), jnp.bfloat16)
    return pl.pallas_call(
        functools.partial(extract_kernel, reach),
        out_shape=(
            jax.ShapeDtypeStruct((3 * labels.shape[0] + 4 * TEMP_HEADS,), jnp.int32),
            jax.ShapeDtypeStruct((1,), jnp.int32),
            pair,
        ),
        in_specs=[HBM] * 4,
        out_specs=(SMEM, SMEM, VMEM),
        scratch_shapes=[
            pltpu.SMEM(labels.shape, jnp.int32),
            pltpu.SMEM(band.shape, jnp.int32),
            pltpu.SMEM((TEMP_HEADS + 1,), jnp.int32),
            pltpu.SemaphoreType.DMA((3,)),
        ],
        compiler_params=pltpu.CompilerParams(vmem_limit_bytes=58 * MIB),
        cost_estimate=pl.CostEstimate(flops=0, bytes_accessed=8 * TEMP_HEADS * half * HEAD_DIM * 2, transcendentals=0),
        name="extract_temporal",
    )(labels, band, keys, values)


def sends_kernel(meta, keys, values, high_send, low_send, sems):
    heads = (meta.shape[0] - 4 * TEMP_HEADS) // 3
    half = high_send.shape[2]
    side, _ = position()
    sent = rows_of(1 - side, half)
    for number in range(TEMP_HEADS):
        columns = columns_of(meta[heads + number])
        block = high_send.at[number] if number < HIGH else low_send.at[number - HIGH]
        for kind, source in enumerate((keys, values)):
            copy = pltpu.make_async_copy(source.at[sent, columns], block.at[kind], sems.at[0 if number < HIGH else 1])
            copy.start()
    for number, whole in enumerate((high_send, low_send)):
        pltpu.make_async_copy(whole, whole, sems.at[number]).wait()


def extract_sends(meta, keys, values):
    half = keys.shape[0] // 2
    outs = [
        jax.ShapeDtypeStruct((count, 2, half, HEAD_DIM), jnp.bfloat16) for count in (HIGH, TEMP_HEADS - HIGH)
    ]
    return pl.pallas_call(
        sends_kernel,
        out_shape=tuple(outs),
        in_specs=[SMEM, HBM, HBM],
        out_specs=(VMEM, VMEM),
        scratch_shapes=[pltpu.SemaphoreType.DMA((2,))],
        compiler_params=pltpu.CompilerParams(vmem_limit_bytes=50 * MIB),
        cost_estimate=pl.CostEstimate(flops=0, bytes_accessed=4 * TEMP_HEADS * half * HEAD_DIM * 2, transcendentals=0),
        name="extract_sends",
    )(meta, keys, values)


def queries_kernel(meta, queries, query_keep, query_send, sems):
    heads = (meta.shape[0] - 4 * TEMP_HEADS) // 3
    half = query_keep.shape[1]
    side, _ = position()
    kept, sent = rows_of(side, half), rows_of(1 - side, half)
    for number in range(TEMP_HEADS):
        columns = columns_of(meta[heads + number])
        pltpu.make_async_copy(queries.at[kept, columns], query_keep.at[number], sems.at[0]).start()
        pltpu.make_async_copy(queries.at[sent, columns], query_send.at[number], sems.at[1]).start()
    for number, whole in enumerate((query_keep, query_send)):
        pltpu.make_async_copy(whole, whole, sems.at[number]).wait()


def extract_queries(meta, queries):
    half = queries.shape[0] // 2
    single = jax.ShapeDtypeStruct((TEMP_HEADS, half, HEAD_DIM), jnp.bfloat16)
    return pl.pallas_call(
        queries_kernel,
        out_shape=(single, single),
        in_specs=[SMEM, HBM],
        out_specs=(VMEM, VMEM),
        scratch_shapes=[pltpu.SemaphoreType.DMA((2,))],
        compiler_params=pltpu.CompilerParams(vmem_limit_bytes=50 * MIB),
        cost_estimate=pl.CostEstimate(flops=0, bytes_accessed=4 * TEMP_HEADS * half * HEAD_DIM * 2, transcendentals=0),
        name="extract_queries",
    )(meta, queries)


def spatial_kernel(scale, first, meta, *refs):
    heads = [refs[5 * number : 5 * number + 5] for number in range(STEP_HEADS)]
    out, held, sems = refs[-3:]
    step, steps = pl.program_id(0), pl.num_programs(0)
    slot = step % 2
    rows = held.shape[2]
    half = rows // 2

    def store(step, slot, number):
        columns = columns_of(meta[first + step * STEP_HEADS + number])
        return pltpu.make_async_copy(held.at[slot, number], out.at[:, columns], sems.at[slot, number])

    @pl.when(step >= 2)
    def _():
        for number in range(STEP_HEADS):
            store(step - 2, slot, number).wait()

    key = [jnp.concatenate([key_own[...], key_far[...]], axis=0) for _, key_own, _, key_far, _ in heads]
    value = [jnp.concatenate([value_own[...], value_far[...]], axis=0) for _, _, value_own, _, value_far in heads]
    parts = [(number, slice(start, start + half)) for number in range(STEP_HEADS) for start in (0, half)]
    scores = [
        lax.dot_general(
            heads[number][0][part, :], key[number], (((1,), (1,)), ((), ())), preferred_element_type=jnp.float32
        )
        for number, part in parts
    ]
    for (number, part), score in zip(parts, scores):
        peak = jnp.max(score, axis=1, keepdims=True)
        weights = jnp.exp2((score - peak) * scale)
        total = jnp.sum(weights, axis=1, keepdims=True)
        result = jnp.dot(weights.astype(jnp.bfloat16), value[number], preferred_element_type=jnp.float32)
        held[slot, number, part, :] = (result / total).astype(jnp.bfloat16)
    for number in range(STEP_HEADS):
        store(step, slot, number).start()

    @pl.when(step == steps - 1)
    def _():
        for number in range(STEP_HEADS):
            store(step, slot, number).wait()

    @pl.when((step == steps - 1) & (steps >= 2))
    def _():
        for number in range(STEP_HEADS):
            store(step - 1, 1 - slot, number).wait()


def spatial_piece(meta, first, count, queries, keys, values, keys_far, values_far, so_far):
    rows = queries.shape[0]
    operands, specs = [], []
    for number in range(STEP_HEADS):
        place = lambda i, meta, number=number: (0, meta[first + i * STEP_HEADS + number])
        operands += [queries, keys, values, keys_far, values_far]
        specs += [pl.BlockSpec((rows, HEAD_DIM), place)] * 5
    aliases = {}
    if so_far is not None:
        operands.append(so_far)
        specs.append(HBM)
        aliases = {len(operands): 0}
    return pl.pallas_call(
        functools.partial(spatial_kernel, math.log2(math.e) / math.sqrt(HEAD_DIM), first),
        out_shape=jax.ShapeDtypeStruct(queries.shape, jnp.bfloat16),
        grid_spec=pltpu.PrefetchScalarGridSpec(
            num_scalar_prefetch=1,
            grid=(count // STEP_HEADS,),
            in_specs=specs,
            out_specs=HBM,
            scratch_shapes=[
                pltpu.VMEM((2, STEP_HEADS, rows, HEAD_DIM), jnp.bfloat16),
                pltpu.SemaphoreType.DMA((2, STEP_HEADS)),
            ],
        ),
        input_output_aliases=aliases,
        compiler_params=pltpu.CompilerParams(vmem_limit_bytes=50 * MIB),
        cost_estimate=pl.CostEstimate(
            flops=count * rows * 2 * rows * HEAD_DIM * 4,
            bytes_accessed=count * 6 * rows * HEAD_DIM * 2,
            transcendentals=count * rows * 2 * rows,
        ),
        name="spatial_heads",
    )(meta, *operands)


def pack_kernel(reach, meta, own_a, low_a, own_b, low_b, for_a, for_b, sems):
    heads = (meta.shape[0] - 4 * TEMP_HEADS) // 3
    side, place = position()
    even = place % 2 == 0
    sources = (
        (jnp.where(even, place + reach - 1, place - reach + 1), own_a, low_a, for_b, sems.at[0]),
        (jnp.where(even, place - reach + 1, place + reach - 1), own_b, low_b, for_a, sems.at[1]),
    )

    def one_item(number, carry):
        item = meta[3 * heads + number]
        head, kind = item // 2, item % 2
        for origin, own, low, out, sem in sources:
            near = (origin < reach).astype(jnp.int32)
            is_own = (near + kind + side) % 2 == 0

            @pl.when(is_own)
            def _():
                pltpu.make_async_copy(own.at[HIGH + head], out.at[number], sem).start()

            @pl.when(jnp.logical_not(is_own))
            def _():
                pltpu.make_async_copy(low.at[head], out.at[number], sem).start()

        return carry

    lax.fori_loop(0, for_a.shape[0], one_item, jnp.int32(0))
    pltpu.make_async_copy(for_a, for_a, sems.at[1]).wait()
    pltpu.make_async_copy(for_b, for_b, sems.at[0]).wait()


def pack(meta, reach, size, own, low):
    out = jax.ShapeDtypeStruct((size,) + low[0].shape[1:], jnp.bfloat16)
    return pl.pallas_call(
        functools.partial(pack_kernel, reach),
        out_shape=(out, out),
        in_specs=[SMEM] + [HBM] * 4,
        out_specs=(VMEM, VMEM),
        scratch_shapes=[pltpu.SemaphoreType.DMA((2,))],
        compiler_params=pltpu.CompilerParams(vmem_limit_bytes=12 * MIB),
        name="pack_items",
    )(meta, own[0], low[0], own[1], low[1])


def temporal_kernel(scale, frames, reach, first_head, stores, meta, query_own, query_far, *rest):
    if stores:
        refs, (_, out, out_far, out_own, sem) = rest[:-5], rest[-5:]
    else:
        refs, (out_own, out_far) = rest[:-2], rest[-2:]
    count, half = out_far.shape[:2]
    is_high = first_head < HIGH
    heads = (meta.shape[0] - 4 * TEMP_HEADS) // 3
    first_listed = 0 if is_high else HIGH
    side, place = position()
    odd = place % 2 == 1
    size = PIXEL_BLOCK

    shifts = [jnp.int32(0)]
    for distance in range(1, reach):
        up = jnp.where(odd, -distance, distance)
        shifts += [up, -up]
    pairs, last = refs[: 2 * len(shifts)], refs[2 * len(shifts) :]
    lower = place < reach
    from_a = lower != odd
    if last:
        shifts.append(jnp.where(lower, reach, -reach))
    slots = 2 * len(shifts)
    row = lax.broadcasted_iota(jnp.int32, (2 * size, 1), 0)
    column = lax.broadcasted_iota(jnp.int32, (1, slots * size), 1)
    row_frame = jnp.where(row >= size, 1 - side, side) + 2 * place
    slot = column // size
    shift = jnp.zeros_like(slot)
    for number, step in enumerate(shifts):
        shift = jnp.where(slot // 2 == number, step, shift)
    first_of = side
    if last and not is_high:
        first_of = jnp.where(slot // 2 == len(shifts) - 1, jnp.where(lower, 0, 1), side)
    column_frame = jnp.where(slot % 2 == 1, 1 - first_of, first_of) + 2 * (place + shift)
    far = 4 * frames
    column_frame = jnp.where((column_frame >= 0) & (column_frame < frames), column_frame, far)
    apart = jnp.where(row % size == column % size, jnp.abs(row_frame - column_frame), far)
    parts = [slice(start, start + size) for start in range(0, half, size)]

    def one_head(number, carry):
        head = first_head + number
        keep = apart <= meta[2 * heads + head]

        def stacked(kind, part):
            blocks = [pair[head if pair.shape[0] == TEMP_HEADS else head - first_listed, kind, part, :] for pair in pairs]
            if is_high:
                for by_b, by_a in (last[:2], last[2:]):
                    blocks.append(jnp.where(from_a, by_a[head, kind, part, :], by_b[head, kind, part, :]))
            elif last:
                for which in range(2):
                    item = meta[3 * heads + 2 * TEMP_HEADS + 2 * (head - HIGH) + which]
                    item = jnp.minimum(item, last[0].shape[0] - 1)
                    by_a, by_b = (block[item, kind, part, :] for block in last)
                    blocks.append(jnp.where(from_a, by_a, by_b))
            return jnp.concatenate(blocks, axis=0)

        scores = []
        for part in parts:
            query = jnp.concatenate([query_own[head, part, :], query_far[head, part, :]], axis=0)
            score = lax.dot_general(
                query, stacked(0, part), (((1,), (1,)), ((), ())), preferred_element_type=jnp.float32
            )
            scores.append(jnp.where(keep, score, MASKED))
        weights = []
        for score in scores:
            peak = jnp.max(score, axis=1, keepdims=True)
            weight = jnp.exp2((score - peak) * scale)
            weights.append((weight.astype(jnp.bfloat16), jnp.sum(weight, axis=1, keepdims=True)))
        results = [
            jnp.dot(weight, stacked(1, part), preferred_element_type=jnp.float32) / total
            for part, (weight, total) in zip(parts, weights)
        ]
        for part, result in zip(parts, results):
            out_own[number, part, :] = result[:size].astype(jnp.bfloat16)
            out_far[number, part, :] = result[size:].astype(jnp.bfloat16)
        if stores:
            columns = columns_of(meta[heads + head])
            pltpu.make_async_copy(out_own.at[number], out.at[rows_of(side, half), columns], sem).start()
        return carry

    lax.fori_loop(0, count, one_head, jnp.int32(0))
    if stores:
        pltpu.make_async_copy(out_own, out_own, sem).wait()


def temporal(meta, frames, reach, heads, query_own, query_far, pairs, last, so_far=None):
    first_head, end = heads
    count, half = end - first_head, query_own.shape[1]
    stores = so_far is not None
    operands = [meta, query_own, query_far, *pairs, *last]
    specs = [SMEM] + [VMEM] * (len(operands) - 1)
    block = jax.ShapeDtypeStruct((count, half, HEAD_DIM), jnp.bfloat16)
    outs, out_specs, scratch = (block, block), (VMEM, VMEM), []
    if stores:
        operands.append(so_far)
        specs.append(HBM)
        outs, out_specs = (jax.ShapeDtypeStruct(so_far.shape, so_far.dtype), block), (HBM, VMEM)
        scratch = [pltpu.VMEM(block.shape, block.dtype), pltpu.SemaphoreType.DMA(())]
    slots = 2 + len(pairs)
    return pl.pallas_call(
        functools.partial(
            temporal_kernel, math.log2(math.e) / math.sqrt(HEAD_DIM), frames, reach, first_head, stores
        ),
        out_shape=outs,
        in_specs=specs,
        out_specs=out_specs,
        scratch_shapes=scratch,
        input_output_aliases={len(operands) - 1: 0} if stores else {},
        compiler_params=pltpu.CompilerParams(vmem_limit_bytes=44 * MIB),
        cost_estimate=pl.CostEstimate(
            flops=count * half * slots * PIXEL_BLOCK * HEAD_DIM * 8,
            bytes_accessed=count * half * HEAD_DIM * 2 * (4 + 2 * slots),
            transcendentals=count * half * 2 * slots * PIXEL_BLOCK,
        ),
        name="temporal_heads",
    )(*operands)


def finish_kernel(plan, meta, *refs):
    blocks, (_, out, sem) = refs[:-3], refs[-3:]
    heads = (meta.shape[0] - 4 * TEMP_HEADS) // 3
    side, _ = position()
    for block, (head, came_back) in zip(blocks, plan):
        count, half = block.shape[:2]
        rows = rows_of(1 - side if came_back else side, half)
        for number in range(count):
            columns = columns_of(meta[heads + head + number])
            pltpu.make_async_copy(block.at[number], out.at[rows, columns], sem).start()
    for block in blocks:
        pltpu.make_async_copy(block, block, sem).wait()


def finish(meta, parts, so_far):
    blocks = [block for block, _, _ in parts]
    return pl.pallas_call(
        functools.partial(finish_kernel, [(head, came_back) for _, head, came_back in parts]),
        out_shape=jax.ShapeDtypeStruct(so_far.shape, so_far.dtype),
        in_specs=[SMEM] + [VMEM] * len(blocks) + [HBM],
        out_specs=HBM,
        scratch_shapes=[pltpu.SemaphoreType.DMA(())],
        input_output_aliases={1 + len(blocks): 0},
        compiler_params=pltpu.CompilerParams(vmem_limit_bytes=4 * MIB),
        cost_estimate=pl.CostEstimate(flops=0, bytes_accessed=so_far.size // 2, transcendentals=0),
        name="finish",
    )(meta, *blocks, so_far)


def shards(queries, keys, values, labels, band):
    frames = lax.axis_size("frame") // 2
    reach = frames // 4

    keys_far = swap_bit(keys, 0)
    values_far = swap_bit(values, 0)
    meta, choice, pair_keep = extract(reach, labels, band, keys, values)
    high_send, low_send = extract_sends(meta, keys, values)

    def attend_piece(result, number):
        first, count = sum(SPATIAL_PIECES[:number]), SPATIAL_PIECES[number]
        return spatial_piece(meta, first, count, queries, keys, values, keys_far, values_far, result)

    def both_swaps(held, distance):
        return swap_pairs(held[1], 0, distance), swap_pairs(held[0], 1, distance)

    own = both_swaps((pair_keep, pair_keep), 1)
    high_got = swap_bit(high_send, 1)
    low_got = swap_bit(low_send, 1)
    result = attend_piece(None, 0)
    meta_then, result = lax.optimization_barrier((meta, result))
    query_keep, query_send = extract_queries(meta_then, queries)
    high_got, query_send, result = lax.optimization_barrier((high_got, query_send, result))
    high = both_swaps((high_got, high_got), 1)
    result = attend_piece(result, 1)
    own, low_got, query_send, choice, result = lax.optimization_barrier((own, low_got, query_send, choice, result))
    low = both_swaps((low_got, low_got), 1)
    high_pairs = [pair_keep, high_got, own[0], high[0], own[1], high[1]]
    low_pairs = [pair_keep, low_got, own[0], low[0], own[1], low[1]]
    for distance in range(2, reach):
        own, high, low = (both_swaps(held, distance) for held in (own, high, low))
        high_pairs += [own[0], high[0], own[1], high[1]]
        low_pairs += [own[0], low[0], own[1], low[1]]
    own_last = both_swaps((own[0][:HIGH], own[1][:HIGH]), reach)
    own_last = own_last[::-1]
    high, result = lax.optimization_barrier((high, result))
    choice = largest(choice)
    query_got = swap_bit(query_send, 1)
    result = attend_piece(result, 2)
    own, high, low, own_last, query_got, choice, result = lax.optimization_barrier(
        (own, high, low, own_last, query_got, choice, result)
    )

    def last_swaps(size, result, meta, own, high, low, own_last, query_keep, query_got, high_pairs, low_pairs):
        attend = functools.partial(temporal, meta, frames, reach)
        high_last = both_swaps(high, reach)
        with_items = min(HIGH + size, TEMP_HEADS)
        parts = []
        if with_items < TEMP_HEADS:
            result, send = attend((with_items, TEMP_HEADS), query_keep, query_got, low_pairs, [], result)
            parts.append((swap_bit(send, 1), with_items, True))
            meta_then, query_keep, _ = lax.optimization_barrier((meta, query_keep, send))
        else:
            meta_then = meta
        if size:
            for_a, for_b = pack(meta_then, reach, size, own, low)
            items = [swap_pairs(for_a, 0, reach), swap_pairs(for_b, 1, reach)]
        keep, send = attend((0, HIGH), query_keep, query_got, high_pairs, [*own_last, *high_last[::-1]])
        parts += [(keep, 0, False), (swap_bit(send, 1), 0, True)]
        if size:
            query_keep, *_ = lax.optimization_barrier((query_keep, send, [block for block, _, _ in parts[:-1]]))
            keep, send = attend((HIGH, with_items), query_keep, query_got, low_pairs, items)
            parts += [(keep, HIGH, False), (swap_bit(send, 1), HIGH, True)]
        return finish(meta, parts, result)

    return lax.switch(
        choice[0], [functools.partial(last_swaps, size) for size in LEVELS],
        result, meta, own, high, low, own_last, query_keep, query_got, high_pairs, low_pairs,
    )


def solution(mesh):
    placed = (
        P(("group", "frame"), None),
        P(("group", "frame"), None),
        P(("group", "frame"), None),
        P("group"),
        P("group"),
    )
    return jax.shard_map(
        shards, mesh=mesh, in_specs=placed, out_specs=P(("group", "frame"), None), check_vma=False
    )
```

```python
import functools
import math

import jax
import jax.numpy as jnp
from jax import lax
from jax.experimental import pallas as pl
from jax.experimental.pallas import tpu as pltpu
from jax.sharding import PartitionSpec as P

TEMP_HEADS = 10
HEAD_DIM = 128
PIXEL_BLOCK = 32
SPATIAL_PIECES = (12, 3, 15)
STEP_HEADS = 3
HIGH = 5
LEVELS = (0, 2, 3, 4, 5, 6, 2 * (TEMP_HEADS - HIGH))
MASKED = -1e30
MIB = 1024 * 1024
HBM = pl.BlockSpec(memory_space=pltpu.HBM)
SMEM = pl.BlockSpec(memory_space=pltpu.SMEM)
VMEM = pl.BlockSpec(memory_space=pltpu.VMEM)


def swap_bit(block, bit):
    count = lax.axis_size("frame")
    return lax.ppermute(block, "frame", [(i, i ^ (1 << bit)) for i in range(count)])


def swap_pairs(block, first, distance):
    count = lax.axis_size("frame")
    places = count // 4
    route = []
    for low in range(first, places - 1, 2):
        if low - (distance - 1) >= 0:
            route += [(low * 4 + i, low * 4 + 4 + i) for i in range(4)]
        if low + distance < places:
            route += [(low * 4 + 4 + i, low * 4 + i) for i in range(4)]
    return lax.ppermute(block, "frame", route)


def largest(value):
    count = lax.axis_size("group")
    result = value
    for shift in range(1, count):
        route = [(i, (i + shift) % count) for i in range(count)]
        result = jnp.maximum(result, lax.ppermute(value, "group", route))
    return result


def position():
    index = lax.axis_index("frame")
    return (index // 2) % 2, index // 4


def columns_of(head):
    return pl.ds(pl.multiple_of(head * HEAD_DIM, HEAD_DIM), HEAD_DIM)


def rows_of(side, half):
    return pl.ds(pl.multiple_of(side * half, half), half)


def extract_kernel(
    reach, labels_hbm, band_hbm, keys, values,
    meta, choice, pair_keep, labels, band, found, sems,
):
    heads = labels.shape[0]
    half = pair_keep.shape[2]
    side, _ = position()
    small = [
        pltpu.make_async_copy(labels_hbm, labels, sems.at[0]),
        pltpu.make_async_copy(band_hbm, band, sems.at[1]),
    ]
    for copy in small:
        copy.start()
    for copy in small:
        copy.wait()

    temporal = jnp.int32(0)
    for head in range(heads):
        found[temporal] = head
        temporal = temporal + labels[head]
    listed_heads = [found[number] for number in range(TEMP_HEADS)]
    bands = [band[head] for head in listed_heads]
    kept = rows_of(side, half)
    for number, head in enumerate(listed_heads):
        rank = jnp.int32(0)
        for other in range(TEMP_HEADS):
            if other != number:
                before = bands[other] >= bands[number] if other < number else bands[other] > bands[number]
                rank = rank + before.astype(jnp.int32)
        meta[heads + rank] = head
        meta[2 * heads + rank] = bands[number]
        columns = columns_of(head)
        for kind, source in enumerate((keys, values)):
            pltpu.make_async_copy(source.at[kept, columns], pair_keep.at[rank, kind], sems.at[2]).start()

    spatial = jnp.int32(0)
    for head in range(heads):
        meta[spatial] = head
        spatial = jnp.minimum(spatial + 1 - labels[head], heads - TEMP_HEADS)
    items = 3 * heads
    places = items + 2 * TEMP_HEADS
    for number in range(2 * TEMP_HEADS):
        meta[items + number] = 0
    listed = jnp.int32(0)
    for number in range(TEMP_HEADS - HIGH):
        for kind in range(2):
            is_needed = meta[2 * heads + HIGH + number] >= 2 * reach - 1 + kind
            meta[places + 2 * number + kind] = listed

            @pl.when(is_needed)
            def _():
                meta[items + listed] = 2 * number + kind

            listed = listed + is_needed.astype(jnp.int32)
    choice[0] = sum((listed > level).astype(jnp.int32) for level in LEVELS[:-1])
    pltpu.make_async_copy(pair_keep, pair_keep, sems.at[2]).wait()


def extract(reach, labels, band, keys, values):
    half = keys.shape[0] // 2
    pair = jax.ShapeDtypeStruct((TEMP_HEADS, 2, half, HEAD_DIM), jnp.bfloat16)
    return pl.pallas_call(
        functools.partial(extract_kernel, reach),
        out_shape=(
            jax.ShapeDtypeStruct((3 * labels.shape[0] + 4 * TEMP_HEADS,), jnp.int32),
            jax.ShapeDtypeStruct((1,), jnp.int32),
            pair,
        ),
        in_specs=[HBM] * 4,
        out_specs=(SMEM, SMEM, VMEM),
        scratch_shapes=[
            pltpu.SMEM(labels.shape, jnp.int32),
            pltpu.SMEM(band.shape, jnp.int32),
            pltpu.SMEM((TEMP_HEADS + 1,), jnp.int32),
            pltpu.SemaphoreType.DMA((3,)),
        ],
        compiler_params=pltpu.CompilerParams(vmem_limit_bytes=58 * MIB),
        cost_estimate=pl.CostEstimate(flops=0, bytes_accessed=8 * TEMP_HEADS * half * HEAD_DIM * 2, transcendentals=0),
        name="extract_temporal",
    )(labels, band, keys, values)


def sends_kernel(meta, keys, values, high_send, low_send, sems):
    heads = (meta.shape[0] - 4 * TEMP_HEADS) // 3
    half = high_send.shape[2]
    side, _ = position()
    sent = rows_of(1 - side, half)
    for number in range(TEMP_HEADS):
        columns = columns_of(meta[heads + number])
        block = high_send.at[number] if number < HIGH else low_send.at[number - HIGH]
        for kind, source in enumerate((keys, values)):
            copy = pltpu.make_async_copy(source.at[sent, columns], block.at[kind], sems.at[0 if number < HIGH else 1])
            copy.start()
    for number, whole in enumerate((high_send, low_send)):
        pltpu.make_async_copy(whole, whole, sems.at[number]).wait()


def extract_sends(meta, keys, values):
    half = keys.shape[0] // 2
    outs = [
        jax.ShapeDtypeStruct((count, 2, half, HEAD_DIM), jnp.bfloat16) for count in (HIGH, TEMP_HEADS - HIGH)
    ]
    return pl.pallas_call(
        sends_kernel,
        out_shape=tuple(outs),
        in_specs=[SMEM, HBM, HBM],
        out_specs=(VMEM, VMEM),
        scratch_shapes=[pltpu.SemaphoreType.DMA((2,))],
        compiler_params=pltpu.CompilerParams(vmem_limit_bytes=50 * MIB),
        cost_estimate=pl.CostEstimate(flops=0, bytes_accessed=4 * TEMP_HEADS * half * HEAD_DIM * 2, transcendentals=0),
        name="extract_sends",
    )(meta, keys, values)


def queries_kernel(meta, queries, query_keep, query_send, sems):
    heads = (meta.shape[0] - 4 * TEMP_HEADS) // 3
    half = query_keep.shape[1]
    side, _ = position()
    kept, sent = rows_of(side, half), rows_of(1 - side, half)
    for number in range(TEMP_HEADS):
        columns = columns_of(meta[heads + number])
        pltpu.make_async_copy(queries.at[kept, columns], query_keep.at[number], sems.at[0]).start()
        pltpu.make_async_copy(queries.at[sent, columns], query_send.at[number], sems.at[1]).start()
    for number, whole in enumerate((query_keep, query_send)):
        pltpu.make_async_copy(whole, whole, sems.at[number]).wait()


def extract_queries(meta, queries):
    half = queries.shape[0] // 2
    single = jax.ShapeDtypeStruct((TEMP_HEADS, half, HEAD_DIM), jnp.bfloat16)
    return pl.pallas_call(
        queries_kernel,
        out_shape=(single, single),
        in_specs=[SMEM, HBM],
        out_specs=(VMEM, VMEM),
        scratch_shapes=[pltpu.SemaphoreType.DMA((2,))],
        compiler_params=pltpu.CompilerParams(vmem_limit_bytes=50 * MIB),
        cost_estimate=pl.CostEstimate(flops=0, bytes_accessed=4 * TEMP_HEADS * half * HEAD_DIM * 2, transcendentals=0),
        name="extract_queries",
    )(meta, queries)


def spatial_kernel(scale, first, meta, *refs):
    heads = [refs[5 * number : 5 * number + 5] for number in range(STEP_HEADS)]
    out, held, sems = refs[-3:]
    step, steps = pl.program_id(0), pl.num_programs(0)
    slot = step % 2
    rows = held.shape[2]
    half = rows // 2

    def store(step, slot, number):
        columns = columns_of(meta[first + step * STEP_HEADS + number])
        return pltpu.make_async_copy(held.at[slot, number], out.at[:, columns], sems.at[slot, number])

    @pl.when(step >= 2)
    def _():
        for number in range(STEP_HEADS):
            store(step - 2, slot, number).wait()

    key = [jnp.concatenate([key_own[...], key_far[...]], axis=0) for _, key_own, _, key_far, _ in heads]
    value = [jnp.concatenate([value_own[...], value_far[...]], axis=0) for _, _, value_own, _, value_far in heads]
    parts = [(number, slice(start, start + half)) for number in range(STEP_HEADS) for start in (0, half)]
    scores = [
        lax.dot_general(
            heads[number][0][part, :], key[number], (((1,), (1,)), ((), ())), preferred_element_type=jnp.float32
        )
        for number, part in parts
    ]
    for (number, part), score in zip(parts, scores):
        peak = jnp.max(score, axis=1, keepdims=True)
        weights = jnp.exp2((score - peak) * scale)
        total = jnp.sum(weights, axis=1, keepdims=True)
        result = jnp.dot(weights.astype(jnp.bfloat16), value[number], preferred_element_type=jnp.float32)
        held[slot, number, part, :] = (result / total).astype(jnp.bfloat16)
    for number in range(STEP_HEADS):
        store(step, slot, number).start()

    @pl.when(step == steps - 1)
    def _():
        for number in range(STEP_HEADS):
            store(step, slot, number).wait()

    @pl.when((step == steps - 1) & (steps >= 2))
    def _():
        for number in range(STEP_HEADS):
            store(step - 1, 1 - slot, number).wait()


def spatial_piece(meta, first, count, queries, keys, values, keys_far, values_far, so_far):
    rows = queries.shape[0]
    operands, specs = [], []
    for number in range(STEP_HEADS):
        place = lambda i, meta, number=number: (0, meta[first + i * STEP_HEADS + number])
        operands += [queries, keys, values, keys_far, values_far]
        specs += [pl.BlockSpec((rows, HEAD_DIM), place)] * 5
    aliases = {}
    if so_far is not None:
        operands.append(so_far)
        specs.append(HBM)
        aliases = {len(operands): 0}
    return pl.pallas_call(
        functools.partial(spatial_kernel, math.log2(math.e) / math.sqrt(HEAD_DIM), first),
        out_shape=jax.ShapeDtypeStruct(queries.shape, jnp.bfloat16),
        grid_spec=pltpu.PrefetchScalarGridSpec(
            num_scalar_prefetch=1,
            grid=(count // STEP_HEADS,),
            in_specs=specs,
            out_specs=HBM,
            scratch_shapes=[
                pltpu.VMEM((2, STEP_HEADS, rows, HEAD_DIM), jnp.bfloat16),
                pltpu.SemaphoreType.DMA((2, STEP_HEADS)),
            ],
        ),
        input_output_aliases=aliases,
        compiler_params=pltpu.CompilerParams(vmem_limit_bytes=50 * MIB),
        cost_estimate=pl.CostEstimate(
            flops=count * rows * 2 * rows * HEAD_DIM * 4,
            bytes_accessed=count * 6 * rows * HEAD_DIM * 2,
            transcendentals=count * rows * 2 * rows,
        ),
        name="spatial_heads",
    )(meta, *operands)


def pack_kernel(reach, meta, own_a, low_a, own_b, low_b, for_a, for_b, sems):
    heads = (meta.shape[0] - 4 * TEMP_HEADS) // 3
    side, place = position()
    even = place % 2 == 0
    sources = (
        (jnp.where(even, place + reach - 1, place - reach + 1), own_a, low_a, for_b, sems.at[0]),
        (jnp.where(even, place - reach + 1, place + reach - 1), own_b, low_b, for_a, sems.at[1]),
    )

    def one_item(number, carry):
        item = meta[3 * heads + number]
        head, kind = item // 2, item % 2
        for origin, own, low, out, sem in sources:
            near = (origin < reach).astype(jnp.int32)
            is_own = (near + kind + side) % 2 == 0

            @pl.when(is_own)
            def _():
                pltpu.make_async_copy(own.at[HIGH + head], out.at[number], sem).start()

            @pl.when(jnp.logical_not(is_own))
            def _():
                pltpu.make_async_copy(low.at[head], out.at[number], sem).start()

        return carry

    lax.fori_loop(0, for_a.shape[0], one_item, jnp.int32(0))
    pltpu.make_async_copy(for_a, for_a, sems.at[1]).wait()
    pltpu.make_async_copy(for_b, for_b, sems.at[0]).wait()


def pack(meta, reach, size, own, low):
    out = jax.ShapeDtypeStruct((size,) + low[0].shape[1:], jnp.bfloat16)
    return pl.pallas_call(
        functools.partial(pack_kernel, reach),
        out_shape=(out, out),
        in_specs=[SMEM] + [HBM] * 4,
        out_specs=(VMEM, VMEM),
        scratch_shapes=[pltpu.SemaphoreType.DMA((2,))],
        compiler_params=pltpu.CompilerParams(vmem_limit_bytes=12 * MIB),
        name="pack_items",
    )(meta, own[0], low[0], own[1], low[1])


def temporal_kernel(scale, frames, reach, first_head, stores, meta, query_own, query_far, *rest):
    if stores:
        refs, (_, out, out_far, out_own, sem) = rest[:-5], rest[-5:]
    else:
        refs, (out_own, out_far) = rest[:-2], rest[-2:]
    count, half = out_far.shape[:2]
    is_high = first_head < HIGH
    heads = (meta.shape[0] - 4 * TEMP_HEADS) // 3
    first_listed = 0 if is_high else HIGH
    side, place = position()
    odd = place % 2 == 1
    size = PIXEL_BLOCK

    shifts = [jnp.int32(0)]
    for distance in range(1, reach):
        up = jnp.where(odd, -distance, distance)
        shifts += [up, -up]
    pairs, last = refs[: 2 * len(shifts)], refs[2 * len(shifts) :]
    lower = place < reach
    from_a = lower != odd
    if last:
        shifts.append(jnp.where(lower, reach, -reach))
    slots = 2 * len(shifts)
    row = lax.broadcasted_iota(jnp.int32, (2 * size, 1), 0)
    column = lax.broadcasted_iota(jnp.int32, (1, slots * size), 1)
    row_frame = jnp.where(row >= size, 1 - side, side) + 2 * place
    slot = column // size
    shift = jnp.zeros_like(slot)
    for number, step in enumerate(shifts):
        shift = jnp.where(slot // 2 == number, step, shift)
    first_of = side
    if last and not is_high:
        first_of = jnp.where(slot // 2 == len(shifts) - 1, jnp.where(lower, 0, 1), side)
    column_frame = jnp.where(slot % 2 == 1, 1 - first_of, first_of) + 2 * (place + shift)
    far = 4 * frames
    column_frame = jnp.where((column_frame >= 0) & (column_frame < frames), column_frame, far)
    apart = jnp.where(row % size == column % size, jnp.abs(row_frame - column_frame), far)
    parts = [slice(start, start + size) for start in range(0, half, size)]

    def one_head(number, carry):
        head = first_head + number
        keep = apart <= meta[2 * heads + head]

        def stacked(kind, part):
            blocks = [pair[head if pair.shape[0] == TEMP_HEADS else head - first_listed, kind, part, :] for pair in pairs]
            if is_high:
                for by_b, by_a in (last[:2], last[2:]):
                    blocks.append(jnp.where(from_a, by_a[head, kind, part, :], by_b[head, kind, part, :]))
            elif last:
                for which in range(2):
                    item = meta[3 * heads + 2 * TEMP_HEADS + 2 * (head - HIGH) + which]
                    item = jnp.minimum(item, last[0].shape[0] - 1)
                    by_a, by_b = (block[item, kind, part, :] for block in last)
                    blocks.append(jnp.where(from_a, by_a, by_b))
            return jnp.concatenate(blocks, axis=0)

        scores = []
        for part in parts:
            query = jnp.concatenate([query_own[head, part, :], query_far[head, part, :]], axis=0)
            score = lax.dot_general(
                query, stacked(0, part), (((1,), (1,)), ((), ())), preferred_element_type=jnp.float32
            )
            scores.append(jnp.where(keep, score, MASKED))
        weights = []
        for score in scores:
            peak = jnp.max(score, axis=1, keepdims=True)
            weight = jnp.exp2((score - peak) * scale)
            weights.append((weight.astype(jnp.bfloat16), jnp.sum(weight, axis=1, keepdims=True)))
        results = [
            jnp.dot(weight, stacked(1, part), preferred_element_type=jnp.float32) / total
            for part, (weight, total) in zip(parts, weights)
        ]
        for part, result in zip(parts, results):
            out_own[number, part, :] = result[:size].astype(jnp.bfloat16)
            out_far[number, part, :] = result[size:].astype(jnp.bfloat16)
        if stores:
            columns = columns_of(meta[heads + head])
            pltpu.make_async_copy(out_own.at[number], out.at[rows_of(side, half), columns], sem).start()
        return carry

    lax.fori_loop(0, count, one_head, jnp.int32(0))
    if stores:
        pltpu.make_async_copy(out_own, out_own, sem).wait()


def temporal(meta, frames, reach, heads, query_own, query_far, pairs, last, so_far=None):
    first_head, end = heads
    count, half = end - first_head, query_own.shape[1]
    stores = so_far is not None
    operands = [meta, query_own, query_far, *pairs, *last]
    specs = [SMEM] + [VMEM] * (len(operands) - 1)
    block = jax.ShapeDtypeStruct((count, half, HEAD_DIM), jnp.bfloat16)
    outs, out_specs, scratch = (block, block), (VMEM, VMEM), []
    if stores:
        operands.append(so_far)
        specs.append(HBM)
        outs, out_specs = (jax.ShapeDtypeStruct(so_far.shape, so_far.dtype), block), (HBM, VMEM)
        scratch = [pltpu.VMEM(block.shape, block.dtype), pltpu.SemaphoreType.DMA(())]
    slots = 2 + len(pairs)
    return pl.pallas_call(
        functools.partial(
            temporal_kernel, math.log2(math.e) / math.sqrt(HEAD_DIM), frames, reach, first_head, stores
        ),
        out_shape=outs,
        in_specs=specs,
        out_specs=out_specs,
        scratch_shapes=scratch,
        input_output_aliases={len(operands) - 1: 0} if stores else {},
        compiler_params=pltpu.CompilerParams(vmem_limit_bytes=44 * MIB),
        cost_estimate=pl.CostEstimate(
            flops=count * half * slots * PIXEL_BLOCK * HEAD_DIM * 8,
            bytes_accessed=count * half * HEAD_DIM * 2 * (4 + 2 * slots),
            transcendentals=count * half * 2 * slots * PIXEL_BLOCK,
        ),
        name="temporal_heads",
    )(*operands)


def finish_kernel(plan, meta, *refs):
    blocks, (_, out, sem) = refs[:-3], refs[-3:]
    heads = (meta.shape[0] - 4 * TEMP_HEADS) // 3
    side, _ = position()
    for block, (head, came_back) in zip(blocks, plan):
        count, half = block.shape[:2]
        rows = rows_of(1 - side if came_back else side, half)
        for number in range(count):
            columns = columns_of(meta[heads + head + number])
            pltpu.make_async_copy(block.at[number], out.at[rows, columns], sem).start()
    for block in blocks:
        pltpu.make_async_copy(block, block, sem).wait()


def finish(meta, parts, so_far):
    blocks = [block for block, _, _ in parts]
    return pl.pallas_call(
        functools.partial(finish_kernel, [(head, came_back) for _, head, came_back in parts]),
        out_shape=jax.ShapeDtypeStruct(so_far.shape, so_far.dtype),
        in_specs=[SMEM] + [VMEM] * len(blocks) + [HBM],
        out_specs=HBM,
        scratch_shapes=[pltpu.SemaphoreType.DMA(())],
        input_output_aliases={1 + len(blocks): 0},
        compiler_params=pltpu.CompilerParams(vmem_limit_bytes=4 * MIB),
        cost_estimate=pl.CostEstimate(flops=0, bytes_accessed=so_far.size // 2, transcendentals=0),
        name="finish",
    )(meta, *blocks, so_far)


def shards(queries, keys, values, labels, band):
    frames = lax.axis_size("frame") // 2
    reach = frames // 4

    keys_far = swap_bit(keys, 0)
    values_far = swap_bit(values, 0)
    meta, choice, pair_keep = extract(reach, labels, band, keys, values)
    high_send, low_send = extract_sends(meta, keys, values)

    def attend_piece(result, number):
        first, count = sum(SPATIAL_PIECES[:number]), SPATIAL_PIECES[number]
        return spatial_piece(meta, first, count, queries, keys, values, keys_far, values_far, result)

    def both_swaps(held, distance):
        return swap_pairs(held[1], 0, distance), swap_pairs(held[0], 1, distance)

    own = both_swaps((pair_keep, pair_keep), 1)
    high_got = swap_bit(high_send, 1)
    low_got = swap_bit(low_send, 1)
    result = attend_piece(None, 0)
    meta_then, result = lax.optimization_barrier((meta, result))
    query_keep, query_send = extract_queries(meta_then, queries)
    high_got, query_send, result = lax.optimization_barrier((high_got, query_send, result))
    high = both_swaps((high_got, high_got), 1)
    result = attend_piece(result, 1)
    own, low_got, query_send, choice, result = lax.optimization_barrier((own, low_got, query_send, choice, result))
    low = both_swaps((low_got, low_got), 1)
    high_pairs = [pair_keep, high_got, own[0], high[0], own[1], high[1]]
    low_pairs = [pair_keep, low_got, own[0], low[0], own[1], low[1]]
    for distance in range(2, reach):
        own, high, low = (both_swaps(held, distance) for held in (own, high, low))
        high_pairs += [own[0], high[0], own[1], high[1]]
        low_pairs += [own[0], low[0], own[1], low[1]]
    own_last = both_swaps((own[0][:HIGH], own[1][:HIGH]), reach)
    own_last = own_last[::-1]
    high, result = lax.optimization_barrier((high, result))
    choice = largest(choice)
    query_got = swap_bit(query_send, 1)
    result = attend_piece(result, 2)
    own, high, low, own_last, query_got, choice, result = lax.optimization_barrier(
        (own, high, low, own_last, query_got, choice, result)
    )

    def last_swaps(size, result, meta, own, high, low, own_last, query_keep, query_got, high_pairs, low_pairs):
        attend = functools.partial(temporal, meta, frames, reach)
        high_last = both_swaps(high, reach)
        with_items = min(HIGH + size, TEMP_HEADS)
        parts = []
        if with_items < TEMP_HEADS:
            result, send = attend((with_items, TEMP_HEADS), query_keep, query_got, low_pairs, [], result)
            parts.append((swap_bit(send, 1), with_items, True))
            meta_then, query_keep, _ = lax.optimization_barrier((meta, query_keep, send))
        else:
            meta_then = meta
        if size:
            for_a, for_b = pack(meta_then, reach, size, own, low)
            items = [swap_pairs(for_a, 0, reach), swap_pairs(for_b, 1, reach)]
        keep, send = attend((0, HIGH), query_keep, query_got, high_pairs, [*own_last, *high_last[::-1]])
        parts += [(keep, 0, False), (swap_bit(send, 1), 0, True)]
        if size:
            query_keep, *_ = lax.optimization_barrier((query_keep, send, [block for block, _, _ in parts[:-1]]))
            keep, send = attend((HIGH, with_items), query_keep, query_got, low_pairs, items)
            parts += [(keep, HIGH, False), (swap_bit(send, 1), HIGH, True)]
        return finish(meta, parts, result)

    return lax.switch(
        choice[0], [functools.partial(last_swaps, size) for size in LEVELS],
        result, meta, own, high, low, own_last, query_keep, query_got, high_pairs, low_pairs,
    )


def solution(mesh):
    placed = (
        P(("group", "frame"), None),
        P(("group", "frame"), None),
        P(("group", "frame"), None),
        P("group"),
        P("group"),
    )
    return jax.shard_map(
        shards, mesh=mesh, in_specs=placed, out_specs=P(("group", "frame"), None), check_vma=False
    )
```
